512 devices in a mesh: ctx: 32 (over z, core), tp: 4 (over y), dp: 4 (over x).
Axes of the slice: x: 4, y: 4, z: 16, core: 2. Of those that a mesh axis runs over, the one named last changes fastest.
Arguments:
- q_raw: bfloat16 [4, 4096, 4096], P('dp', 'ctx', 'tp'), may hold values from -30 to 30
- k_raw: bfloat16 [4, 4096, 512], P('dp', 'ctx', 'tp'), may hold values from -30 to 30
- values_in: bfloat16 [4, 4096, 512], P('dp', 'ctx', 'tp'), may hold values from -6 to 6
- grad_out: bfloat16 [4, 4096, 4096], P('dp', 'ctx', 'tp'), may hold values from -15 to 15
- q_gain: float32 [128], replicated, may hold values from 0.5 to 5.5
- k_gain: float32 [128], replicated, may hold values from 0.5 to 5.5
Outputs:
- d_q: bfloat16 [4, 4096, 4096], P('dp', 'ctx', 'tp')
- d_k: bfloat16 [4, 4096, 512], P('dp', 'ctx', 'tp')
- d_v: bfloat16 [4, 4096, 512], P('dp', 'ctx', 'tp')
- gain_grads: float32 [2, 128], replicated
The draws below stay inside these ranges and needn't reach their ends.
All inputs are finite; a program needn't handle non-finite values.
Results may differ from the reference program's by a relative error of at most 0.009.
The reference program's roundings to bfloat16 on the way count: a program that leaves them out, or rounds other values in their place, can miss the bound.
Values may be sent and summed in bfloat16 or wider, within the bound.
A program may use at most 64 MiB of HBM per device.

```python
import jax
import jax.numpy as jnp
from jax import lax

HD = 128
KVH = 4
HQ = 32
SEQ = 4096
BATCH = 4


def key_field(key):
    base_noise = jnp.clip(jax.random.normal(key, (BATCH, SEQ, KVH, HD), jnp.float32), -5.0, 5.0)
    row_scale = jnp.exp(jax.random.uniform(jax.random.fold_in(key, 1), (BATCH, SEQ, KVH, 1), jnp.float32, jnp.log(0.3), jnp.log(3.0)))
    chan_scale = jnp.exp(jax.random.uniform(jax.random.fold_in(key, 2), (1, 1, 1, HD), jnp.float32, jnp.log(0.5), jnp.log(2.0)))
    field = base_noise * row_scale * chan_scale
    return jnp.clip(field, -30.0, 30.0)


def draw_k_raw(key, part):
    field = key_field(key)
    return field.reshape(BATCH, SEQ, KVH * HD).astype(jnp.bfloat16)


def draw_q_raw(key, part):
    key = jax.random.fold_in(key, 5)
    base_noise = jnp.clip(jax.random.normal(key, (BATCH, SEQ, HQ, HD), jnp.float32), -5.0, 5.0)
    row_scale = jnp.exp(jax.random.uniform(jax.random.fold_in(key, 1), (BATCH, SEQ, HQ, 1), jnp.float32, jnp.log(0.3), jnp.log(3.0)))
    chan_scale = jnp.exp(jax.random.uniform(jax.random.fold_in(key, 2), (1, 1, 1, HD), jnp.float32, jnp.log(0.5), jnp.log(2.0)))
    queries = base_noise * row_scale * chan_scale
    return jnp.clip(queries, -30.0, 30.0).reshape(BATCH, SEQ, HQ * HD).astype(jnp.bfloat16)


def draw_grad_out(key, part):
    key = jax.random.fold_in(key, 9)
    positions = jnp.arange(SEQ, dtype=jnp.float32)
    ramp = (1.0 + 2.0 * positions / SEQ)[None, :, None]
    base_noise = jnp.clip(jax.random.normal(key, (BATCH, SEQ, HQ * HD), jnp.float32), -5.0, 5.0)
    return (base_noise * ramp).astype(jnp.bfloat16)


def draw_q_gain(key, part):
    key = jax.random.fold_in(key, 7)
    gains = jnp.exp(jax.random.uniform(key, (HD,), jnp.float32, jnp.log(0.5), jnp.log(2.5)))
    return gains


def draw_k_gain(key, part):
    key = jax.random.fold_in(key, 8)
    gains = jnp.exp(jax.random.uniform(key, (HD,), jnp.float32, jnp.log(0.5), jnp.log(2.5)))
    return gains


def steps_of(key, shape, split, smallest, top_value):
    level = 1.0
    for position, parts in split:
        heights = jax.random.uniform(jax.random.fold_in(jax.random.fold_in(key, 6), position), (parts,), jnp.float32, smallest / len(split), top_value / len(split))
        level = level * jnp.repeat(jnp.exp(heights), shape[position] // parts).reshape((-1,) + (1,) * (len(shape) - 1 - position))
    return level


def gaussian(stream_key, shape, scale, bound, pieces=(), kind=jnp.bfloat16):
    loudness = steps_of(stream_key, shape, pieces, -0.22, 0.18) if pieces else 1.0
    result = jax.random.normal(stream_key, shape, jnp.float32) * scale * loudness
    return jnp.minimum(jnp.maximum(result, -bound), bound).astype(kind)


def setup_inputs(seed: int = 0) -> dict:
    splits = jax.random.split(jax.random.key(seed), 7)
    return {
        "q_raw": draw_q_raw(jax.random.fold_in(splits[6], 71), 0),
        "k_raw": draw_k_raw(jax.random.fold_in(splits[6], 71), 0),
        "values_in": gaussian(splits[2], (BATCH, SEQ, KVH * HD), 1.0, 6.0, ((0, 4), (1, 32), (2, 4))),
        "grad_out": draw_grad_out(jax.random.fold_in(splits[6], 71), 0),
        "q_gain": draw_q_gain(jax.random.fold_in(splits[6], 71), 0),
        "k_gain": draw_k_gain(jax.random.fold_in(splits[6], 71), 0),
    }


eps = 1e-06
masked = -1e+30

def normalize(raw, gain):
    values = raw.astype(jnp.float32).reshape(raw.shape[0], -1, HD)
    inverse = lax.rsqrt(lax.optimization_barrier(jnp.mean(values * values, axis=2, keepdims=True)) + eps)
    return (values, inverse, (values * inverse * gain).astype(jnp.bfloat16))

def norm_back(values, inverse, gain, upstream):
    scaled = gain * upstream
    inner = lax.optimization_barrier(jnp.mean(scaled * values, axis=2, keepdims=True))
    grad_in = inverse * scaled - values * (inverse * inverse * inverse) * inner
    gain_part = lax.optimization_barrier(jnp.sum(upstream * values * inverse, axis=(0, 1)))
    return (grad_in, gain_part)

def reference(q_raw, k_raw, values_in, grad_out, q_gain, k_gain):
    score_scale = HD ** (-0.5)
    group_size = HQ // KVH
    positions = jnp.arange(SEQ, dtype=jnp.int32)
    allowed = positions[None, :] <= positions[:, None]
    q_outputs, k_outputs, v_outputs = ([], [], [])
    q_gain_total = jnp.zeros((HD,), jnp.float32)
    k_gain_total = jnp.zeros((HD,), jnp.float32)
    for seq_index in range(BATCH):
        q_vals, q_inv, q_norm = normalize(q_raw[seq_index], q_gain)
        k_vals, k_inv, k_norm = normalize(k_raw[seq_index], k_gain)
        value_heads = values_in[seq_index].reshape(SEQ, KVH, HD)
        upstream = grad_out[seq_index].reshape(SEQ, HQ, HD)

        def one_head(head_index):
            kv_index = head_index // group_size
            query = q_norm[:, head_index]
            keys = k_norm[:, kv_index]
            vals = value_heads[:, kv_index]
            cotan = upstream[:, head_index]
            scores = jnp.dot(query, keys.T, preferred_element_type=jnp.float32) * score_scale
            scores = jnp.where(allowed, scores, masked)
            row_max = lax.optimization_barrier(jnp.max(scores, axis=1))
            row_mass = lax.optimization_barrier(jnp.sum(jnp.where(allowed, jnp.exp(scores - row_max[:, None]), 0.0), axis=1))
            lse = row_max + jnp.log(row_mass)
            prob = jnp.where(allowed, jnp.exp(scores - lse[:, None]), 0.0)
            dprob = jnp.dot(cotan, vals.T, preferred_element_type=jnp.float32)
            delta = lax.optimization_barrier(jnp.sum(prob * dprob, axis=1))
            dscore = prob * (dprob - delta[:, None])
            prob_b = prob.astype(jnp.bfloat16)
            dscore_b = dscore.astype(jnp.bfloat16)
            grad_vals = jnp.dot(prob_b.T, cotan, preferred_element_type=jnp.float32)
            grad_keys = score_scale * jnp.dot(dscore_b.T, query, preferred_element_type=jnp.float32)
            grad_query = score_scale * jnp.dot(dscore_b, keys, preferred_element_type=jnp.float32)
            return (grad_query, grad_keys, grad_vals)
        grad_query, grad_keys, grad_vals = lax.map(one_head, jnp.arange(HQ, dtype=jnp.int32))
        grad_query = jnp.transpose(grad_query, (1, 0, 2))
        grad_keys = jnp.transpose(grad_keys.reshape(KVH, group_size, SEQ, HD).sum(axis=1), (1, 0, 2))
        grad_vals = jnp.transpose(grad_vals.reshape(KVH, group_size, SEQ, HD).sum(axis=1), (1, 0, 2))
        q_grad, q_part = norm_back(q_vals, q_inv, q_gain, grad_query)
        k_grad, k_part = norm_back(k_vals, k_inv, k_gain, grad_keys)
        q_gain_total = q_gain_total + q_part
        k_gain_total = k_gain_total + k_part
        q_outputs.append(q_grad.reshape(SEQ, HQ * HD).astype(jnp.bfloat16))
        k_outputs.append(k_grad.reshape(SEQ, KVH * HD).astype(jnp.bfloat16))
        v_outputs.append(grad_vals.reshape(SEQ, KVH * HD).astype(jnp.bfloat16))
    gain_grads = jnp.stack([q_gain_total, k_gain_total])
    return (jnp.stack(q_outputs), jnp.stack(k_outputs), jnp.stack(v_outputs), gain_grads)
```

```python
import functools
import math

import jax
import jax.numpy as jnp
from jax import lax
from jax.experimental import pallas as pl
from jax.experimental.pallas import tpu as pltpu
from jax.sharding import PartitionSpec as P

HD = 128
CW = 256
EPS = 1e-06
MASKED = -1e30
F32 = jnp.float32
BF16 = jnp.bfloat16
MESH = pl.DeviceIdType.MESH


def dot(a, b, contract):
    return lax.dot_general(
        a, b, (((contract[0],), (contract[1],)), ((), ())), preferred_element_type=F32
    )


def inverse_rms(x):
    return lax.rsqrt(jnp.mean(x * x, axis=1, keepdims=True) + EPS)


def norm_back(x, inv, gain, upstream):
    scaled = gain * upstream
    inner = jnp.mean(scaled * x, axis=1, keepdims=True)
    grad = inv * scaled - x * (inv * inv * inv) * inner
    return grad, jnp.sum(upstream * x * inv, axis=0, keepdims=True)


def first_pass(kv, qh, go, probs, dprobs, block_max, stats, zo, core, diagonal, scale2):
    keys = kv[pl.ds(2 * zo, 2), 0].reshape(2 * HD, HD)
    vals = kv[pl.ds(2 * zo, 2), 1].reshape(2 * HD, HD)
    total = qh.shape[0]
    for start in range(0, total, CW):
        cols = slice(start, start + CW)
        s = dot(keys, qh[cols, :], (1, 1))
        if diagonal:
            key_pos = lax.broadcasted_iota(jnp.int32, (2 * HD, CW), 0)
            query_pos = core * HD + lax.broadcasted_iota(jnp.int32, (2 * HD, CW), 1) % HD
            s = jnp.where(key_pos <= query_pos, s, MASKED)
        dp = dot(vals, go[cols, :], (1, 1))
        top = jnp.max(s, axis=0, keepdims=True)
        if not diagonal:
            old = stats[0:1, cols]
            top = jnp.maximum(top, old)
        p = jnp.exp2(s * scale2 - top * scale2)
        mass = jnp.sum(p, axis=0, keepdims=True)
        weighted = jnp.sum(p * dp, axis=0, keepdims=True)
        if not diagonal:
            shrink = jnp.exp2((old - top) * scale2)
            mass += stats[1:2, cols] * shrink
            weighted += stats[2:3, cols] * shrink
        stats[0:1, cols] = top
        stats[1:2, cols] = mass
        stats[2:3, cols] = weighted
        block_max[zo, :, cols] = top
        probs[zo, :, cols] = p
        dprobs[zo, :, cols] = dp


def second_pass(kv, qh, go, probs, dprobs, block_max, stats, prob_b, dscore_b, dq_t, sums, zo, scale2):
    total = qh.shape[0]
    keys = kv[pl.ds(2 * zo, 2), 0].reshape(2 * HD, HD)
    for start in range(0, total, CW):
        cols = slice(start, start + CW)
        factor = jnp.exp2((block_max[zo, :, cols] - stats[0:1, cols]) * scale2) * stats[1:2, cols]
        p = probs[zo, :, cols] * factor
        ds = p * (dprobs[zo, :, cols] - stats[2:3, cols])
        prob_b[:, cols] = p.astype(BF16)
        ds = ds.astype(BF16)
        dscore_b[:, cols] = ds
        dq_t[:, cols] += dot(keys, ds, (0, 0))
    sums[0] = dot(dscore_b[...], qh[...], (1, 0)).reshape(2, HD, HD)
    sums[1] = dot(prob_b[...], go[...], (1, 0)).reshape(2, HD, HD)


def kernel(
    n, tp, dp,
    q_hbm, k_hbm, v_hbm, g_hbm, q_gain, k_gain,
    dq_hbm, dk_out, dv_out, gains_out,
    q_raw, k_raw, qh, go, kv, probs, dprobs, block_max, stats, prob_b, dscore_b, dq_t, dq_out,
    keep, swap_out, swap_in, ring_out, ring_in, line_out, line_in, plane_out, plane_in,
    load_sem, head_sem, store_sem,
    g_send, g_recv, sib_send, sib_recv, r_send, r_recv, swap_send, swap_recv,
    line_send, line_recv, plane_send, plane_recv,
):
    chips, half, heads = n // 2, n // 4, qh.shape[0] // HD
    scale = HD ** (-0.5)
    scale2 = scale * math.log2(math.e)
    me = lax.axis_index("ctx")
    z, core = me // 2, me % 2
    sibling = me + 1 - 2 * core
    place = lax.axis_index("tp") * dp + lax.axis_index("dp")
    group = tp * dp

    barrier = pltpu.get_barrier_semaphore()

    @pl.loop(1, n)
    def _(i):
        pl.semaphore_signal(barrier, 1, device_id={"ctx": (me + i) % n}, device_id_type=MESH)

    @pl.loop(1, group)
    def _(i):
        to = (place + i) % group
        pl.semaphore_signal(barrier, 1, device_id={"tp": to // dp, "dp": to % dp}, device_id_type=MESH)

    def load(i):
        src, dst = ((k_hbm.at[0], k_raw), (v_hbm.at[0], kv.at[me, 1]), (q_hbm.at[0], q_raw))[i]
        return pltpu.make_async_copy(src, dst, load_sem.at[i])

    def load_head(h):
        return pltpu.make_async_copy(
            g_hbm.at[0, :, pl.ds(h * HD, HD)], go.at[pl.ds(h * HD, HD)], head_sem.at[h]
        )

    for i in range(3):
        load(i).start()
    for h in range(heads):
        load_head(h).start()

    load(0).wait()
    x = k_raw[...].astype(F32)
    kv[me, 0] = (x * inverse_rms(x) * k_gain[...]).astype(BF16)
    load(1).wait()

    def ring_copy(direction, owner, index, part, to):
        block = kv.at[2 * owner + core, part]
        return pltpu.make_async_remote_copy(
            block, block, g_send.at[direction, index, part], g_recv.at[direction, index, part],
            device_id={"ctx": 2 * to + core}, device_id_type=MESH,
        )

    def sibling_copy(owner, part, owner_core):
        block = kv.at[2 * owner + owner_core, part]
        return pltpu.make_async_remote_copy(
            block, block, sib_send.at[owner, part], sib_recv.at[owner, part],
            device_id={"ctx": sibling}, device_id_type=MESH,
        )

    pl.semaphore_wait(barrier, n + group - 2)

    first_up = z < chips - 1
    first_around = z <= half - 2
    for part in range(2):
        @pl.when(first_up)
        def _():
            ring_copy(0, z, 0, part, z + 1).start()

        @pl.when(first_around)
        def _():
            ring_copy(1, z, z, part, chips - 1).start()

        sibling_copy(z, part, core).start()

    load(2).wait()
    for h in range(heads):
        cols = slice(h * HD, (h + 1) * HD)
        x = q_raw[:, cols].astype(F32)
        qh[cols, :] = (x * inverse_rms(x) * q_gain[...]).astype(BF16)
    for h in range(heads):
        load_head(h).wait()

    one = functools.partial(
        first_pass, kv, qh, go, probs, dprobs, block_max, stats, core=core, scale2=scale2
    )
    two = functools.partial(
        second_pass, kv, qh, go, probs, dprobs, block_max, stats, prob_b, dscore_b, dq_t, scale2=scale2
    )

    for part in range(2):
        sibling_copy(z, part, 1 - core).wait_recv()
    one(zo=z, diagonal=True)

    def gathered(direction, step):
        owner = jnp.where(direction == 0, z - 1 - step, step)
        limit = jnp.where(direction == 0, z, z - half)
        return owner, step < limit

    def forwarded(direction, step):
        to = jnp.where(direction == 0, z + 1, z - 1)
        index = jnp.where(direction == 0, step + 1, step)
        limit = jnp.where(direction == 0, jnp.where(z < chips - 1, half - 1, 0), z - half - 1)
        return to, index, step < limit

    @pl.loop(0, half + 1)
    def _(step):
        @pl.when(step < half)
        def _():
            @pl.loop(0, 2)
            def _(direction):
                owner, comes = gathered(direction, step)
                to, index, goes = forwarded(direction, step)

                @pl.when(comes)
                def _():
                    for part in range(2):
                        ring_copy(direction, owner, step, part, to).wait_recv()

                        @pl.when(goes)
                        def _():
                            ring_copy(direction, owner, index, part, to).start()

                        sibling_copy(owner, part, core).start()

        @pl.when(step >= 1)
        def _():
            @pl.loop(0, 2)
            def _(direction):
                owner, comes = gathered(direction, step - 1)

                @pl.when(comes)
                def _():
                    for part in range(2):
                        sibling_copy(owner, part, 1 - core).wait_recv()
                    one(zo=owner, diagonal=False)

    inv_mass = 1.0 / stats[1:2, :]
    stats[2:3, :] = stats[2:3, :] * inv_mass
    stats[1:2, :] = inv_mass
    dq_t[...] = jnp.zeros_like(dq_t)

    def owed(direction, step):
        owner = jnp.where(direction == 0, z - half + step, z - half - 1 - step)
        last = jnp.where(direction == 0, half, half - 2)
        return owner, jnp.logical_and(owner >= 0, step <= last)

    def swap(owner):
        return pltpu.make_async_remote_copy(
            swap_out.at[owner], swap_in.at[owner], swap_send.at[owner], swap_recv.at[owner],
            device_id={"ctx": sibling}, device_id_type=MESH,
        )

    def pass_on(direction, owner, index, part):
        around = jnp.where(z == chips - 1, owner, z + 1)
        to = jnp.where(direction == 0, z - 1, around)
        return pltpu.make_async_remote_copy(
            ring_out.at[direction, index, part], ring_in.at[direction, index, part],
            r_send.at[direction, index, part], r_recv.at[direction, index, part],
            device_id={"ctx": 2 * to + core}, device_id_type=MESH,
        )

    @pl.loop(0, half + 1)
    def _(step):
        @pl.loop(0, 2)
        def _(direction):
            owner, valid = owed(direction, step)

            @pl.when(valid)
            def _():
                sums = keep.at[step % 2, direction]
                two(sums=sums, zo=owner)
                for part in range(2):
                    swap_out[owner, part] = sums[part, 1 - core].astype(swap_out.dtype)
                swap(owner).start()

        @pl.when(step >= 1)
        def _():
            before = step - 1

            @pl.loop(0, 2)
            def _(direction):
                owner, valid = owed(direction, before)

                @pl.when(valid)
                def _():
                    swap(owner).wait_recv()
                    arrives = jnp.logical_and(before >= 1, jnp.logical_or(direction == 1, z < chips - 1))
                    index = jnp.maximum(before - 1, 0)
                    for part in range(2):
                        here = keep.at[before % 2, direction, part, core]
                        here[...] += swap_in[owner, part].astype(F32)

                        @pl.when(arrives)
                        def _():
                            pass_on(direction, owner, index, part).wait_recv()
                            here[...] += ring_in[direction, index, part].astype(F32)

                        ring_out[direction, before, part] = here[...].astype(BF16)
                        pass_on(direction, owner, before, part).start()

    q_part = jnp.zeros((1, HD), F32)
    for h in range(heads):
        cols = slice(h * HD, (h + 1) * HD)
        x = q_raw[:, cols].astype(F32)
        upstream = scale * dq_t[:, cols].T
        grad, part = norm_back(x, inverse_rms(x), q_gain[...], upstream)
        q_part += part
        dq_out[:, cols] = grad.astype(BF16)
    store = pltpu.make_async_copy(dq_out, dq_hbm.at[0], store_sem)
    store.start()

    swap(z).wait_recv()
    for part in range(2):
        here = keep.at[half % 2, 0, part, core]
        here[...] += swap_in[z, part].astype(F32)

        @pl.when(z < chips - 1)
        def _():
            pass_on(0, z, half - 1, part).wait_recv()
            here[...] += ring_in[0, half - 1, part].astype(F32)

        @pl.when(z <= half - 2)
        def _():
            index = jnp.maximum(half - 2 - z, 0)
            pass_on(1, z, index, part).wait_recv()
            here[...] += ring_in[1, index, part].astype(F32)

    x = k_raw[...].astype(F32)
    upstream = scale * keep[half % 2, 0, 0, core]
    grad, k_part = norm_back(x, inverse_rms(x), k_gain[...], upstream)
    dk_out[0] = grad.astype(BF16)
    dv_out[0] = keep[half % 2, 0, 1, core].astype(BF16)

    def line_copy(i):
        to = (me + i) % n
        return pltpu.make_async_remote_copy(
            line_out, line_in.at[me], line_send.at[i], line_recv.at[me],
            device_id={"ctx": to}, device_id_type=MESH,
        )

    def line_arrival(i):
        source = (me + i) % n
        return pltpu.make_async_remote_copy(
            line_out, line_in.at[source], line_send.at[i], line_recv.at[source],
            device_id={"ctx": source}, device_id_type=MESH,
        )

    def plane_copy(i, slot):
        to = (place + i) % group
        return pltpu.make_async_remote_copy(
            plane_out, plane_in.at[slot], plane_send.at[i], plane_recv.at[slot],
            device_id={"tp": to // dp, "dp": to % dp}, device_id_type=MESH,
        )

    line_out[0:1] = q_part
    line_out[1:2] = k_part
    line_in[me] = line_out[...]

    @pl.loop(1, n)
    def _(i):
        line_copy(i).start()

    @pl.loop(1, n)
    def _(i):
        line_arrival(i).wait_recv()

    plane_out[...] = jnp.sum(line_in[...], axis=0)
    plane_in[place] = plane_out[...]

    @pl.loop(1, group)
    def _(i):
        plane_copy(i, place).start()

    @pl.loop(1, group)
    def _(i):
        plane_copy(i, (place + i) % group).wait_recv()

    gains_out[...] = jnp.sum(plane_in[...], axis=0)

    for part in range(2):
        @pl.when(first_up)
        def _():
            ring_copy(0, z, 0, part, z + 1).wait_send()

        @pl.when(first_around)
        def _():
            ring_copy(1, z, z, part, chips - 1).wait_send()

        sibling_copy(z, part, core).wait_send()

    @pl.loop(0, half)
    def _(step):
        @pl.loop(0, 2)
        def _(direction):
            owner, comes = gathered(direction, step)
            to, index, goes = forwarded(direction, step)

            @pl.when(comes)
            def _():
                for part in range(2):
                    @pl.when(goes)
                    def _():
                        ring_copy(direction, owner, index, part, to).wait_send()

                    sibling_copy(owner, part, core).wait_send()

            owner, valid = owed(direction, step)

            @pl.when(valid)
            def _():
                swap(owner).wait_send()
                for part in range(2):
                    pass_on(direction, owner, step, part).wait_send()

    swap(z).wait_send()

    @pl.loop(1, n)
    def _(i):
        line_copy(i).wait_send()

    @pl.loop(1, group)
    def _(i):
        plane_copy(i, place).wait_send()

    store.wait()


def solution(mesh):
    n, tp, dp = mesh.shape["ctx"], mesh.shape["tp"], mesh.shape["dp"]
    chips, half = n // 2, n // 4

    def shards(q_raw, k_raw, values_in, grad_out, q_gain, k_gain):
        rows, width = q_raw.shape[1:]
        flat = rows * width // HD
        whole = pl.BlockSpec(memory_space=pltpu.VMEM)
        anywhere = pl.BlockSpec(memory_space=pl.ANY)
        dma = pltpu.SemaphoreType.DMA
        outs = pl.pallas_call(
            functools.partial(kernel, n, tp, dp),
            out_shape=(
                jax.ShapeDtypeStruct(q_raw.shape, BF16),
                jax.ShapeDtypeStruct(k_raw.shape, BF16),
                jax.ShapeDtypeStruct(k_raw.shape, BF16),
                jax.ShapeDtypeStruct((2, HD), F32),
            ),
            in_specs=[anywhere] * 4 + [whole] * 2,
            out_specs=(anywhere, whole, whole, whole),
            scratch_shapes=[
                pltpu.VMEM((rows, width), BF16),
                pltpu.VMEM((rows, HD), BF16),
                pltpu.VMEM((flat, HD), BF16),
                pltpu.VMEM((flat, HD), BF16),
                pltpu.VMEM((n, 2, HD, HD), BF16),
                pltpu.VMEM((chips, 2 * HD, flat), F32),
                pltpu.VMEM((chips, 2 * HD, flat), F32),
                pltpu.VMEM((chips, 1, flat), F32),
                pltpu.VMEM((8, flat), F32),
                pltpu.VMEM((2 * HD, flat), BF16),
                pltpu.VMEM((2 * HD, flat), BF16),
                pltpu.VMEM((HD, flat), F32),
                pltpu.VMEM((rows, width), BF16),
                pltpu.VMEM((2, 2, 2, 2, HD, HD), F32),
                pltpu.VMEM((chips, 2, HD, HD), BF16),
                pltpu.VMEM((chips, 2, HD, HD), BF16),
                pltpu.VMEM((2, half, 2, HD, HD), BF16),
                pltpu.VMEM((2, half, 2, HD, HD), BF16),
                pltpu.VMEM((2, HD), F32),
                pltpu.VMEM((n, 2, HD), F32),
                pltpu.VMEM((2, HD), F32),
                pltpu.VMEM((tp * dp, 2, HD), F32),
                dma((3,)), dma((flat // HD,)), dma,
                dma((2, half, 2)), dma((2, half, 2)),
                dma((chips, 2)), dma((chips, 2)),
                dma((2, half, 2)), dma((2, half, 2)),
                dma((chips,)), dma((chips,)),
                dma((n,)), dma((n,)),
                dma((tp * dp,)), dma((tp * dp,)),
            ],
            compiler_params=pltpu.CompilerParams(
                collective_id=0, has_side_effects=True, vmem_limit_bytes=56 * 1024 * 1024
            ),
            cost_estimate=pl.CostEstimate(
                flops=10 * flat * n * rows * HD, bytes_accessed=6 * rows * width,
                transcendentals=flat * n * rows,
            ),
        )(q_raw, k_raw, values_in, grad_out, q_gain.reshape(1, HD), k_gain.reshape(1, HD))
        return outs

    spread = P("dp", "ctx", "tp")
    return jax.shard_map(
        shards,
        mesh=mesh,
        in_specs=(spread, spread, spread, spread, P(), P()),
        out_specs=(spread, spread, spread, P()),
        check_vma=False,
    )
```

```python
import functools
import math

import jax
import jax.numpy as jnp
from jax import lax
from jax.experimental import pallas as pl
from jax.experimental.pallas import tpu as pltpu
from jax.sharding import PartitionSpec as P

HD = 128
CW = 256
EPS = 1e-06
MASKED = -1e30
F32 = jnp.float32
BF16 = jnp.bfloat16
MESH = pl.DeviceIdType.MESH

GATHER = {0: (1, 2), 2: (3, 4), 4: (5, 6), 6: (7, 8)}
SCATTER = {0: (1, 3), 1: (2,), 3: (4, 6), 4: (5,), 6: (7, 8)}
AROUND = {0: (1, 3), 1: (2,), 3: (4, 6), 4: (5,)}
WRAP = {0: (1, 3), 1: (2,), 3: (4, 5, 6)}
GATHER_ORDER = (2, 1, 4, 3, 6, 5, 8, 7)
SCATTER_ORDER = (8, 7, 5, 2, 6, 4, 1, 3)
AROUND_DELAY = {0: 1, 1: 3, 3: 3, 2: 5, 4: 5, 6: 5, 5: 6}
NEAR = 3


def pick(index, table):
    out = jnp.int32(-1)
    for key, value in table.items():
        out = jnp.where(index == key, value, out)
    return out


def children(tree, reach, slot):
    kept = {d: [c for c in cs if c <= reach] for d, cs in tree.items()}
    return {d: cs[slot] for d, cs in kept.items() if len(cs) > slot}


def height(place, owner, far):
    below = [1 + height(c, owner, far) for c in WRAP.get(place, ()) if owner <= far - c]
    return max(below, default=0)


def parents(tree, reach):
    return {c: d for d, cs in tree.items() for c in cs if c <= reach}


def dot(a, b, contract):
    return lax.dot_general(
        a, b, (((contract[0],), (contract[1],)), ((), ())), preferred_element_type=F32
    )


def inverse_rms(x):
    return lax.rsqrt(jnp.mean(x * x, axis=1, keepdims=True) + EPS)


def norm_back(x, inv, gain, upstream):
    scaled = gain * upstream
    inner = jnp.mean(scaled * x, axis=1, keepdims=True)
    grad = inv * scaled - x * (inv * inv * inv) * inner
    return grad, jnp.sum(upstream * x * inv, axis=0, keepdims=True)


def first_pass(kv, qh, go, probs, dprobs, block_max, stats, zo, core, diagonal, scale2):
    keys = kv[pl.ds(2 * zo, 2), 0].reshape(2 * HD, HD)
    vals = kv[pl.ds(2 * zo, 2), 1].reshape(2 * HD, HD)
    total = qh.shape[0]
    for start in range(0, total, CW):
        cols = slice(start, start + CW)
        s = dot(keys, qh[cols, :], (1, 1))
        if diagonal:
            key_pos = lax.broadcasted_iota(jnp.int32, (2 * HD, CW), 0)
            query_pos = core * HD + lax.broadcasted_iota(jnp.int32, (2 * HD, CW), 1) % HD
            s = jnp.where(key_pos <= query_pos, s, MASKED)
        dp = dot(vals, go[cols, :], (1, 1))
        top = jnp.max(s, axis=0, keepdims=True)
        if not diagonal:
            old = stats[0:1, cols]
            top = jnp.maximum(top, old)
        p = jnp.exp2(s * scale2 - top * scale2)
        mass = jnp.sum(p, axis=0, keepdims=True)
        weighted = jnp.sum(p * dp, axis=0, keepdims=True)
        if not diagonal:
            shrink = jnp.exp2((old - top) * scale2)
            mass += stats[1:2, cols] * shrink
            weighted += stats[2:3, cols] * shrink
        stats[0:1, cols] = top
        stats[1:2, cols] = mass
        stats[2:3, cols] = weighted
        block_max[zo, :, cols] = top
        probs[zo, :, cols] = p
        dprobs[zo, :, cols] = dp


def second_pass(kv, qh, go, probs, dprobs, block_max, stats, prob_b, dscore_b, dq_t, sums, zo, scale2):
    total = qh.shape[0]
    keys = kv[pl.ds(2 * zo, 2), 0].reshape(2 * HD, HD)
    for start in range(0, total, CW):
        cols = slice(start, start + CW)
        factor = jnp.exp2((block_max[zo, :, cols] - stats[0:1, cols]) * scale2) * stats[1:2, cols]
        p = probs[zo, :, cols] * factor
        ds = p * (dprobs[zo, :, cols] - stats[2:3, cols])
        prob_b[:, cols] = p.astype(BF16)
        ds = ds.astype(BF16)
        dscore_b[:, cols] = ds
        dq_t[:, cols] += dot(keys, ds, (0, 0))
    sums[0] = dot(dscore_b[...], qh[...], (1, 0)).reshape(2, HD, HD)
    sums[1] = dot(prob_b[...], go[...], (1, 0)).reshape(2, HD, HD)


def kernel(
    n, tp, dp,
    q_hbm, k_hbm, v_hbm, g_hbm, q_gain, k_gain,
    dq_hbm, dk_out, dv_out, gains_out,
    q_raw, k_raw, qh, go, kv, probs, dprobs, block_max, stats, prob_b, dscore_b, dq_t, dq_out,
    keep, swap_out, swap_in, down_out, down_in, wrap_out, wrap_in,
    pair_out, pair_in, line_out, line_in, plane_out, plane_in,
    load_sem, head_sem, store_sem, word,
    up_send, up_recv, around_send, around_recv, sib_send, sib_recv,
    down_send, down_recv, wrap_send, wrap_recv, swap_send, swap_recv,
    pair_send, pair_recv, line_send, line_recv, plane_send, plane_recv,
):
    chips, heads = n // 2, qh.shape[0] // HD
    reach = chips // 2
    far = chips - reach - 2
    top = chips - 1
    scale = HD ** (-0.5)
    scale2 = scale * math.log2(math.e)
    me = lax.axis_index("ctx")
    z, core = me // 2, me % 2
    sibling = me + 1 - 2 * core
    place = lax.axis_index("tp") * dp + lax.axis_index("dp")
    group = tp * dp
    below_top = top - z

    def chip(to):
        return {"ctx": 2 * to + core}

    def plane(to):
        return {"tp": to // dp, "dp": to % dp}

    barrier = pltpu.get_barrier_semaphore()

    def greet(to):
        pl.semaphore_signal(barrier, 1, device_id=chip(to), device_id_type=MESH)

    greeted = jnp.int32(group)
    for away in range(1, NEAR + 1):
        for to in (z + away, z - away):
            inside = jnp.logical_and(to >= 0, to <= top)
            greeted += jnp.where(inside, 1, 0)

            @pl.when(inside)
            def _():
                greet(to)

    greeted += jnp.where(z <= far, 1, 0)

    @pl.when(z == top)
    def _():
        @pl.loop(0, far + 1)
        def _(i):
            greet(i)

    pl.semaphore_signal(barrier, 1, device_id={"ctx": sibling}, device_id_type=MESH)

    @pl.loop(1, group)
    def _(i):
        pl.semaphore_signal(barrier, 1, device_id=plane((place + i) % group), device_id_type=MESH)

    def load(i):
        src, dst = ((k_hbm.at[0], k_raw), (v_hbm.at[0], kv.at[me, 1]), (q_hbm.at[0], q_raw))[i]
        return pltpu.make_async_copy(src, dst, load_sem.at[i])

    def load_head(h):
        return pltpu.make_async_copy(
            g_hbm.at[0, :, pl.ds(h * HD, HD)], go.at[pl.ds(h * HD, HD)], head_sem.at[h]
        )

    for i in range(3):
        load(i).start()
    for h in range(heads):
        load_head(h).start()

    load(0).wait()
    x = k_raw[...].astype(F32)
    kv[me, 0] = (x * inverse_rms(x) * k_gain[...]).astype(BF16)
    load(1).wait()

    def up_copy(owner, distance, part, to):
        block = kv.at[2 * owner + core, part]
        return pltpu.make_async_remote_copy(
            block, block, up_send.at[distance, part], up_recv.at[distance, part],
            device_id=chip(to), device_id_type=MESH,
        )

    def around_copy(owner, slot, part, to):
        block = kv.at[2 * owner + core, part]
        return pltpu.make_async_remote_copy(
            block, block, around_send.at[owner, slot, part], around_recv.at[owner, part],
            device_id=chip(to), device_id_type=MESH,
        )

    def sibling_copy(owner, owner_core):
        block = kv.at[2 * owner + owner_core]
        return pltpu.make_async_remote_copy(
            block, block, sib_send.at[owner], sib_recv.at[owner],
            device_id={"ctx": sibling}, device_id_type=MESH,
        )

    def each_up_send(distance, part, act):
        for slot in (1, 0):
            child = pick(distance, children(GATHER, reach, slot))
            to = z + child - distance

            @pl.when(jnp.logical_and(child > 0, to <= top))
            def _():
                act(up_copy(z - distance, child, part, to))

    def each_around_send(owner, part, act):
        for slot in (1, 0):
            child = pick(below_top, children(AROUND, far, slot))

            @pl.when(jnp.logical_and(child > 0, owner <= far - child))
            def _():
                act(around_copy(owner, slot, part, top - child))

    def each_own_send(act):
        for part in range(2):
            @pl.when(z <= far)
            def _():
                act(around_copy(z, 0, part, top))

            each_up_send(0, part, act)

        act(sibling_copy(z, core))

    pl.semaphore_wait(barrier, greeted)
    each_own_send(lambda copy: copy.start())

    load(2).wait()
    for h in range(heads):
        cols = slice(h * HD, (h + 1) * HD)
        x = q_raw[:, cols].astype(F32)
        qh[cols, :] = (x * inverse_rms(x) * q_gain[...]).astype(BF16)
    for h in range(heads):
        load_head(h).wait()

    one = functools.partial(
        first_pass, kv, qh, go, probs, dprobs, block_max, stats, core=core, scale2=scale2
    )
    two = functools.partial(
        second_pass, kv, qh, go, probs, dprobs, block_max, stats, prob_b, dscore_b, dq_t, scale2=scale2
    )

    sibling_copy(z, 1 - core).wait_recv()
    one(zo=z, diagonal=True)

    up_table = {i: d for i, d in enumerate(d for d in GATHER_ORDER if d <= reach)}
    delay = pick(below_top, AROUND_DELAY)
    gather_steps = max(reach, 1 + max((far - d) // 2 + late for d, late in AROUND_DELAY.items() if d <= far))
    word_step = jnp.minimum(2 * (below_top // NEAR), gather_steps)

    def gathered(source, step):
        distance = pick(step, up_table)
        up = z - distance
        around = 2 * (step - delay) + source - 1
        up_valid = jnp.logical_and(distance > 0, up >= 0)
        around_valid = jnp.logical_and(
            below_top <= far, jnp.logical_and(step >= delay, around <= far - below_top)
        )
        owner = jnp.where(source == 0, up, around)
        return owner, jnp.logical_or(
            jnp.logical_and(source == 0, up_valid), jnp.logical_and(source >= 1, around_valid)
        )

    def each_passed_on(source, step, arrival, act):
        owner, comes = gathered(source, step)

        @pl.when(jnp.logical_and(comes, source == 0))
        def _():
            for part in range(2):
                if arrival:
                    up_copy(owner, z - owner, part, z).wait_recv()
                each_up_send(z - owner, part, act)

        @pl.when(jnp.logical_and(comes, source >= 1))
        def _():
            for part in range(2):
                if arrival:
                    around_copy(owner, 0, part, z).wait_recv()
                each_around_send(owner, part, act)

        @pl.when(comes)
        def _():
            act(sibling_copy(owner, core))

    @pl.loop(0, gather_steps + 1)
    def _(step):
        @pl.when(step == word_step)
        def _():
            @pl.when(z + NEAR <= top)
            def _():
                pl.semaphore_wait(word, 1)

            @pl.when(z >= NEAR)
            def _():
                pl.semaphore_signal(word, 1, device_id=chip(z - NEAR), device_id_type=MESH)

        @pl.loop(0, 3)
        def _(source):
            each_passed_on(source, step, True, lambda copy: copy.start())
            owner, comes = gathered(source, step - 1)

            @pl.when(comes)
            def _():
                sibling_copy(owner, 1 - core).wait_recv()
                one(zo=owner, diagonal=False)

    inv_mass = 1.0 / stats[1:2, :]
    stats[2:3, :] = stats[2:3, :] * inv_mass
    stats[1:2, :] = inv_mass
    dq_t[...] = jnp.zeros_like(dq_t)

    order = [d for d in SCATTER_ORDER if d <= reach]
    down_table = {i: d for i, d in enumerate(order)}
    down_table[reach] = 0
    down_parent, wrap_parent = parents(SCATTER, reach), parents(WRAP, far)
    wrap_slot = {c: i for cs in WRAP.values() for i, c in enumerate(cs)}

    def owed(direction, step):
        distance = pick(step, down_table)
        down = z - distance
        around = z - reach - 1 - step
        owner = jnp.where(direction == 0, down, around)
        limit = jnp.where(direction == 0, distance >= 0, jnp.logical_and(step >= 0, step <= far))
        return owner, jnp.logical_and(owner >= 0, limit)

    def swap(owner):
        return pltpu.make_async_remote_copy(
            swap_out.at[owner], swap_in.at[owner], swap_send.at[owner], swap_recv.at[owner],
            device_id={"ctx": sibling}, device_id_type=MESH,
        )

    def down_copy(distance, part, to):
        return pltpu.make_async_remote_copy(
            down_out.at[distance, part], down_in.at[distance, part],
            down_send.at[distance, part], down_recv.at[distance, part],
            device_id=chip(to), device_id_type=MESH,
        )

    def wrap_copy(owner, slot, part, to):
        return pltpu.make_async_remote_copy(
            wrap_out.at[owner, part], wrap_in.at[owner, slot, part],
            wrap_send.at[owner, part], wrap_recv.at[owner, slot, part],
            device_id=chip(to), device_id_type=MESH,
        )

    def add_swapped(step, direction, owner):
        swap(owner).wait_recv()
        for part in range(2):
            keep[step, direction, part, core] += swap_in[owner, part].astype(F32)

    def add_down(step, distance, part):
        for slot in range(2):
            child = pick(distance, children(SCATTER, reach, slot))

            @pl.when(jnp.logical_and(child > 0, z + child - distance <= top))
            def _():
                down_copy(child, part, z).wait_recv()
                keep[step, 0, part, core] += down_in[child, part].astype(F32)

    def add_wrap(step, owner, part):
        for slot in range(3):
            child = pick(below_top, children(WRAP, far, slot))

            @pl.when(jnp.logical_and(child > 0, owner <= far - child))
            def _():
                wrap_copy(owner, slot, part, z).wait_recv()
                keep[step, 1, part, core] += wrap_in[owner, slot, part].astype(F32)

    def down_target(distance):
        return z - distance + pick(distance, down_parent)

    def each_wrap_send(owner, part, act):
        for slot in range(3):
            @pl.when(pick(below_top, wrap_slot) == slot)
            def _():
                act(wrap_copy(owner, slot, part, top - pick(below_top, wrap_parent)))

        @pl.when(below_top == 0)
        def _():
            act(wrap_copy(owner, 0, part, owner))

    def finish_down(step):
        owner, valid = owed(0, step)

        @pl.when(valid)
        def _():
            distance = z - owner
            add_swapped(step, 0, owner)
            for part in range(2):
                add_down(step, distance, part)
                down_out[distance, part] = keep[step, 0, part, core].astype(BF16)
                down_copy(distance, part, down_target(distance)).start()

    heights = {(p, e): height(p, e, far) for p in range(far + 1) for e in range(far - p + 1)}
    tallest = max(heights.values())

    def finish_wrap(now):
        step = jnp.int32(-1)
        for tall in range(tallest + 1):
            before = now - 1 - 2 * tall
            owner, valid = owed(1, before)
            keys = {p * chips + e: tall for (p, e), h in heights.items() if h == tall}
            due = jnp.logical_and(valid, pick(below_top * chips + owner, keys) == tall)
            step = jnp.where(due, before, step)
        owner, valid = owed(1, step)

        @pl.when(valid)
        def _():
            add_swapped(step, 1, owner)
            for part in range(2):
                add_wrap(step, owner, part)
                wrap_out[owner, part] = keep[step, 1, part, core].astype(BF16)
                each_wrap_send(owner, part, lambda copy: copy.start())

    @pl.loop(0, reach + 1)
    def _(step):
        @pl.loop(0, 2)
        def _(direction):
            owner, valid = owed(direction, step)

            @pl.when(valid)
            def _():
                sums = keep.at[step, direction]
                two(sums=sums, zo=owner)
                for part in range(2):
                    swap_out[owner, part] = sums[part, 1 - core].astype(BF16)
                swap(owner).start()

            @pl.when(direction == 0)
            def _():
                finish_wrap(step)

            @pl.when(direction == 1)
            def _():
                finish_down(step - 1)

    q_part = jnp.zeros((1, HD), F32)
    for h in range(heads):
        cols = slice(h * HD, (h + 1) * HD)
        x = q_raw[:, cols].astype(F32)
        upstream = scale * dq_t[:, cols].T
        grad, part = norm_back(x, inverse_rms(x), q_gain[...], upstream)
        q_part += part
        dq_out[:, cols] = grad.astype(BF16)
    store = pltpu.make_async_copy(dq_out, dq_hbm.at[0], store_sem)
    store.start()

    pair = pltpu.make_async_remote_copy(
        pair_out, pair_in, pair_send, pair_recv, device_id={"ctx": sibling}, device_id_type=MESH
    )

    def offset(i, count):
        away = (i + 1) // 2
        return count // 2 + jnp.where(i % 2 == 1, -away, away)

    def line_copy(i, slot):
        away = offset(i, chips)
        return pltpu.make_async_remote_copy(
            line_out, line_in.at[slot], line_send.at[i], line_recv.at[slot],
            device_id=chip((z + away) % chips), device_id_type=MESH,
        )

    def plane_copy(i, slot):
        return pltpu.make_async_remote_copy(
            plane_out, plane_in.at[slot], plane_send.at[i], plane_recv.at[slot],
            device_id=plane((place + i + 1) % group), device_id_type=MESH,
        )

    pair_out[...] = q_part
    pair.start()

    @pl.loop(reach + 1, far + 2 + 2 * tallest)
    def _(step):
        finish_wrap(step)

    pair.wait_recv()
    line_out[...] = pair_out[...] + pair_in[...]
    line_in[z] = line_out[...]

    @pl.loop(0, chips - 1)
    def _(i):
        line_copy(i, z).start()

    add_swapped(reach, 0, z)
    for part in range(2):
        add_down(reach, 0, part)

    @pl.when(z <= far)
    def _():
        for part in range(2):
            wrap_copy(z, 0, part, z).wait_recv()
            keep[reach, 0, part, core] += wrap_in[z, 0, part].astype(F32)

    x = k_raw[...].astype(F32)
    upstream = scale * keep[reach, 0, 0, core]
    grad, _ = norm_back(x, inverse_rms(x), k_gain[...], upstream)
    dk_out[0] = grad.astype(BF16)
    dv_out[0] = keep[reach, 0, 1, core].astype(BF16)

    @pl.loop(0, chips - 1)
    def _(i):
        line_copy(i, (z + offset(i, chips)) % chips).wait_recv()

    plane_out[...] = jnp.sum(line_in[...], axis=0)
    plane_in[place] = plane_out[...]

    @pl.loop(0, group - 1)
    def _(i):
        plane_copy(i, place).start()

    @pl.loop(0, group - 1)
    def _(i):
        plane_copy(i, (place + i + 1) % group).wait_recv()

    q_total = jnp.sum(plane_in[...], axis=0)
    gains_out[0:1] = q_total
    gains_out[1:2] = q_total * q_gain[...] / k_gain[...]

    def left(copy):
        copy.wait_send()

    each_own_send(left)

    @pl.loop(0, gather_steps)
    def _(step):
        @pl.loop(0, 3)
        def _(source):
            each_passed_on(source, step, False, left)

    @pl.loop(0, reach + 1)
    def _(step):
        owner, valid = owed(0, step)

        @pl.when(valid)
        def _():
            swap(owner).wait_send()

            @pl.when(owner < z)
            def _():
                for part in range(2):
                    down_copy(z - owner, part, down_target(z - owner)).wait_send()

        around, around_valid = owed(1, step)

        @pl.when(around_valid)
        def _():
            swap(around).wait_send()
            for part in range(2):
                each_wrap_send(around, part, left)

    pair.wait_send()

    @pl.loop(0, chips - 1)
    def _(i):
        line_copy(i, z).wait_send()

    @pl.loop(0, group - 1)
    def _(i):
        plane_copy(i, place).wait_send()

    store.wait()


def solution(mesh):
    n, tp, dp = mesh.shape["ctx"], mesh.shape["tp"], mesh.shape["dp"]
    chips, reach = n // 2, n // 4
    far = chips - reach - 2

    def shards(q_raw, k_raw, values_in, grad_out, q_gain, k_gain):
        rows, width = q_raw.shape[1:]
        flat = rows * width // HD
        whole = pl.BlockSpec(memory_space=pltpu.VMEM)
        anywhere = pl.BlockSpec(memory_space=pl.ANY)
        dma = pltpu.SemaphoreType.DMA
        outs = pl.pallas_call(
            functools.partial(kernel, n, tp, dp),
            out_shape=(
                jax.ShapeDtypeStruct(q_raw.shape, BF16),
                jax.ShapeDtypeStruct(k_raw.shape, BF16),
                jax.ShapeDtypeStruct(k_raw.shape, BF16),
                jax.ShapeDtypeStruct((2, HD), F32),
            ),
            in_specs=[anywhere] * 4 + [whole] * 2,
            out_specs=(anywhere, whole, whole, whole),
            scratch_shapes=[
                pltpu.VMEM((rows, width), BF16),
                pltpu.VMEM((rows, HD), BF16),
                pltpu.VMEM((flat, HD), BF16),
                pltpu.VMEM((flat, HD), BF16),
                pltpu.VMEM((n, 2, HD, HD), BF16),
                pltpu.VMEM((chips, 2 * HD, flat), F32),
                pltpu.VMEM((chips, 2 * HD, flat), F32),
                pltpu.VMEM((chips, 1, flat), F32),
                pltpu.VMEM((8, flat), F32),
                pltpu.VMEM((2 * HD, flat), BF16),
                pltpu.VMEM((2 * HD, flat), BF16),
                pltpu.VMEM((HD, flat), F32),
                pltpu.VMEM((rows, width), BF16),
                pltpu.VMEM((reach + 1, 2, 2, 2, HD, HD), F32),
                pltpu.VMEM((chips, 2, HD, HD), BF16),
                pltpu.VMEM((chips, 2, HD, HD), BF16),
                pltpu.VMEM((reach + 1, 2, HD, HD), BF16),
                pltpu.VMEM((reach + 1, 2, HD, HD), BF16),
                pltpu.VMEM((far + 1, 2, HD, HD), BF16),
                pltpu.VMEM((far + 1, 3, 2, HD, HD), BF16),
                pltpu.VMEM((1, HD), F32),
                pltpu.VMEM((1, HD), F32),
                pltpu.VMEM((1, HD), F32),
                pltpu.VMEM((chips, 1, HD), F32),
                pltpu.VMEM((1, HD), F32),
                pltpu.VMEM((tp * dp, 1, HD), F32),
                dma((3,)), dma((flat // HD,)), dma, pltpu.SemaphoreType.REGULAR,
                dma((reach + 1, 2)), dma((reach + 1, 2)),
                dma((far + 1, 2, 2)), dma((far + 1, 2)),
                dma((chips,)), dma((chips,)),
                dma((reach + 1, 2)), dma((reach + 1, 2)),
                dma((far + 1, 2)), dma((far + 1, 3, 2)),
                dma((chips,)), dma((chips,)),
                dma, dma, dma((chips,)), dma((chips,)),
                dma((tp * dp,)), dma((tp * dp,)),
            ],
            compiler_params=pltpu.CompilerParams(
                collective_id=0, has_side_effects=True, vmem_limit_bytes=60 * 1024 * 1024
            ),
            cost_estimate=pl.CostEstimate(
                flops=10 * flat * n * rows * HD, bytes_accessed=6 * rows * width,
                transcendentals=flat * n * rows,
            ),
        )(q_raw, k_raw, values_in, grad_out, q_gain.reshape(1, HD), k_gain.reshape(1, HD))
        return outs

    spread = P("dp", "ctx", "tp")
    return jax.shard_map(
        shards,
        mesh=mesh,
        in_specs=(spread, spread, spread, spread, P(), P()),
        out_specs=(spread, spread, spread, P()),
        check_vma=False,
    )
```

```python
import functools
import math

import jax
import jax.numpy as jnp
from jax import lax
from jax.experimental import pallas as pl
from jax.experimental.pallas import tpu as pltpu
from jax.sharding import PartitionSpec as P

HD = 128
CW = 256
EPS = 1e-06
MASKED = -1e30
F32 = jnp.float32
BF16 = jnp.bfloat16
MESH = pl.DeviceIdType.MESH

GATHER = {0: (1, 3), 1: (2,), 3: (4, 6), 4: (5,), 6: (7, 8)}
SCATTER = {0: (1, 3), 1: (2,), 3: (4, 6), 4: (5,), 6: (7, 8)}
AROUND = {0: (1, 3), 1: (2,), 3: (4, 6), 4: (5,)}
WRAP = {0: (1, 3), 1: (2,), 3: (4, 5, 6)}
GATHER_ORDER = (1, 3, 2, 4, 6, 5, 7, 8)
SCATTER_ORDER = (8, 7, 5, 2, 6, 4, 1, 3)
AROUND_DELAY = {0: 0, 1: 2, 3: 2, 2: 4, 4: 4, 6: 4, 5: 5}
WRAP_UP = False
WRAP_LAG = (1, 2)
NEAR = 3


def pick(index, table):
    out = jnp.int32(-1)
    for key, value in table.items():
        out = jnp.where(index == key, value, out)
    return out


def children(tree, reach, slot):
    kept = {d: [c for c in cs if c <= reach] for d, cs in tree.items()}
    return {d: cs[slot] for d, cs in kept.items() if len(cs) > slot}


def height(place, owner, far):
    below = [1 + height(c, owner, far) for c in WRAP.get(place, ()) if owner <= far - c]
    return max(below, default=0)


def parents(tree, reach):
    return {c: d for d, cs in tree.items() for c in cs if c <= reach}


def dot(a, b, contract):
    return lax.dot_general(
        a, b, (((contract[0],), (contract[1],)), ((), ())), preferred_element_type=F32
    )


def inverse_rms(x):
    return lax.rsqrt(jnp.mean(x * x, axis=1, keepdims=True) + EPS)


def norm_back(x, inv, gain, upstream):
    scaled = gain * upstream
    inner = jnp.mean(scaled * x, axis=1, keepdims=True)
    grad = inv * scaled - x * (inv * inv * inv) * inner
    return grad, jnp.sum(upstream * x * inv, axis=0, keepdims=True)


def first_pass(kv, qh, go, probs, dprobs, block_max, stats, zo, core, diagonal, scale2):
    keys = kv[pl.ds(2 * zo, 2), 0].reshape(2 * HD, HD)
    vals = kv[pl.ds(2 * zo, 2), 1].reshape(2 * HD, HD)
    total = qh.shape[0]
    for start in range(0, total, CW):
        cols = slice(start, start + CW)
        s = dot(keys, qh[cols, :], (1, 1))
        if diagonal:
            key_pos = lax.broadcasted_iota(jnp.int32, (2 * HD, CW), 0)
            query_pos = core * HD + lax.broadcasted_iota(jnp.int32, (2 * HD, CW), 1) % HD
            s = jnp.where(key_pos <= query_pos, s, MASKED)
        dp = dot(vals, go[cols, :], (1, 1))
        top = jnp.max(s, axis=0, keepdims=True)
        if not diagonal:
            old = stats[0:1, cols]
            top = jnp.maximum(top, old)
        p = jnp.exp2(s * scale2 - top * scale2)
        mass = jnp.sum(p, axis=0, keepdims=True)
        weighted = jnp.sum(p * dp, axis=0, keepdims=True)
        if not diagonal:
            shrink = jnp.exp2((old - top) * scale2)
            mass += stats[1:2, cols] * shrink
            weighted += stats[2:3, cols] * shrink
        stats[0:1, cols] = top
        stats[1:2, cols] = mass
        stats[2:3, cols] = weighted
        block_max[zo, :, cols] = top
        probs[zo, :, cols] = p
        dprobs[zo, :, cols] = dp


def second_pass(kv, qh, go, probs, dprobs, block_max, stats, prob_b, dscore_b, dq_t, sums, zo, scale2):
    total = qh.shape[0]
    keys = kv[pl.ds(2 * zo, 2), 0].reshape(2 * HD, HD)
    for start in range(0, total, CW):
        cols = slice(start, start + CW)
        factor = jnp.exp2((block_max[zo, :, cols] - stats[0:1, cols]) * scale2) * stats[1:2, cols]
        p = probs[zo, :, cols] * factor
        ds = p * (dprobs[zo, :, cols] - stats[2:3, cols])
        prob_b[:, cols] = p.astype(BF16)
        ds = ds.astype(BF16)
        dscore_b[:, cols] = ds
        dq_t[:, cols] += dot(keys, ds, (0, 0))
    sums[0] = dot(dscore_b[...], qh[...], (1, 0)).reshape(2, HD, HD)
    sums[1] = dot(prob_b[...], go[...], (1, 0)).reshape(2, HD, HD)


def kernel(
    n, tp, dp,
    q_hbm, k_hbm, v_hbm, g_hbm, q_gain, k_gain,
    dq_hbm, dk_out, dv_out, gains_out,
    q_raw, k_raw, qh, go, kv, probs, dprobs, block_max, stats, prob_b, dscore_b, dq_t, dq_out,
    keep, swap_out, swap_in, down_out, down_in, wrap_out, wrap_in,
    line_out, line_in, plane_out, plane_in,
    load_sem, head_sem, store_sem, word,
    up_send, up_recv, around_send, around_recv, sib_send, sib_recv,
    down_send, down_recv, wrap_send, wrap_recv, swap_send, swap_recv,
    line_send, line_recv, plane_send, plane_recv,
):
    chips, heads = n // 2, qh.shape[0] // HD
    reach = chips // 2
    far = chips - reach - 2
    top = chips - 1
    scale = HD ** (-0.5)
    scale2 = scale * math.log2(math.e)
    me = lax.axis_index("ctx")
    z, core = me // 2, me % 2
    sibling = me + 1 - 2 * core
    place = lax.axis_index("tp") * dp + lax.axis_index("dp")
    group = tp * dp
    below_top = top - z

    def chip(to):
        return {"ctx": 2 * to + core}

    def plane(to):
        return {"tp": to // dp, "dp": to % dp}

    barrier = pltpu.get_barrier_semaphore()

    def greet(to):
        pl.semaphore_signal(barrier, 1, device_id=chip(to), device_id_type=MESH)

    greeted = jnp.int32(group)
    for away in range(1, NEAR + 1):
        for to in (z + away, z - away):
            inside = jnp.logical_and(to >= 0, to <= top)
            greeted += jnp.where(inside, 1, 0)

            @pl.when(inside)
            def _():
                greet(to)

    greeted += jnp.where(z <= far, 1, 0)

    @pl.when(z == top)
    def _():
        @pl.loop(0, far + 1)
        def _(i):
            greet(i)

    pl.semaphore_signal(barrier, 1, device_id={"ctx": sibling}, device_id_type=MESH)

    @pl.loop(1, group)
    def _(i):
        pl.semaphore_signal(barrier, 1, device_id=plane((place + i) % group), device_id_type=MESH)

    def load(i):
        src, dst = ((k_hbm.at[0], k_raw), (v_hbm.at[0], kv.at[me, 1]), (q_hbm.at[0], q_raw))[i]
        return pltpu.make_async_copy(src, dst, load_sem.at[i])

    def load_head(h):
        return pltpu.make_async_copy(
            g_hbm.at[0, :, pl.ds(h * HD, HD)], go.at[pl.ds(h * HD, HD)], head_sem.at[h]
        )

    for i in range(3):
        load(i).start()
    for h in range(heads):
        load_head(h).start()

    load(0).wait()
    x = k_raw[...].astype(F32)
    kv[me, 0] = (x * inverse_rms(x) * k_gain[...]).astype(BF16)
    load(1).wait()

    def up_copy(owner, distance, part, to):
        block = kv.at[2 * owner + core, part]
        return pltpu.make_async_remote_copy(
            block, block, up_send.at[distance, part], up_recv.at[distance, part],
            device_id=chip(to), device_id_type=MESH,
        )

    def around_copy(owner, slot, part, to):
        block = kv.at[2 * owner + core, part]
        return pltpu.make_async_remote_copy(
            block, block, around_send.at[owner, slot, part], around_recv.at[owner, part],
            device_id=chip(to), device_id_type=MESH,
        )

    def sibling_copy(owner, owner_core):
        block = kv.at[2 * owner + owner_core]
        return pltpu.make_async_remote_copy(
            block, block, sib_send.at[owner], sib_recv.at[owner],
            device_id={"ctx": sibling}, device_id_type=MESH,
        )

    def each_up_send(distance, part, act):
        for slot in (1, 0):
            child = pick(distance, children(GATHER, reach, slot))
            to = z + child - distance

            @pl.when(jnp.logical_and(child > 0, to <= top))
            def _():
                act(up_copy(z - distance, child, part, to))

    def each_around_send(owner, part, act):
        for slot in (1, 0):
            child = pick(below_top, children(AROUND, far, slot))

            @pl.when(jnp.logical_and(child > 0, owner <= far - child))
            def _():
                act(around_copy(owner, slot, part, top - child))

    def each_own_send(act):
        for part in range(2):
            @pl.when(z <= far)
            def _():
                act(around_copy(z, 0, part, top))

            each_up_send(0, part, act)

        act(sibling_copy(z, core))

    pl.semaphore_wait(barrier, greeted)
    each_own_send(lambda copy: copy.start())

    load(2).wait()
    for h in range(heads):
        cols = slice(h * HD, (h + 1) * HD)
        x = q_raw[:, cols].astype(F32)
        qh[cols, :] = (x * inverse_rms(x) * q_gain[...]).astype(BF16)
    for h in range(heads):
        load_head(h).wait()

    one = functools.partial(
        first_pass, kv, qh, go, probs, dprobs, block_max, stats, core=core, scale2=scale2
    )
    two = functools.partial(
        second_pass, kv, qh, go, probs, dprobs, block_max, stats, prob_b, dscore_b, dq_t, scale2=scale2
    )

    sibling_copy(z, 1 - core).wait_recv()
    one(zo=z, diagonal=True)

    up_table = {i: d for i, d in enumerate(d for d in GATHER_ORDER if d <= reach)}
    delay = pick(below_top, AROUND_DELAY)
    gather_steps = max(reach, 1 + max((far - d) // 2 + late for d, late in AROUND_DELAY.items() if d <= far))
    word_step = jnp.minimum(2 * (below_top // NEAR), gather_steps)

    def gathered(source, step):
        distance = pick(step, up_table)
        up = z - distance
        around = 2 * (step - delay) + source - 1
        up_valid = jnp.logical_and(distance > 0, up >= 0)
        around_valid = jnp.logical_and(
            below_top <= far, jnp.logical_and(step >= delay, around <= far - below_top)
        )
        owner = jnp.where(source == 0, up, around)
        return owner, jnp.logical_or(
            jnp.logical_and(source == 0, up_valid), jnp.logical_and(source >= 1, around_valid)
        )

    def each_passed_on(source, step, arrival, act):
        owner, comes = gathered(source, step)

        @pl.when(jnp.logical_and(comes, source == 0))
        def _():
            for part in range(2):
                if arrival:
                    up_copy(owner, z - owner, part, z).wait_recv()
                each_up_send(z - owner, part, act)

        @pl.when(jnp.logical_and(comes, source >= 1))
        def _():
            for part in range(2):
                if arrival:
                    around_copy(owner, 0, part, z).wait_recv()
                each_around_send(owner, part, act)

        @pl.when(comes)
        def _():
            act(sibling_copy(owner, core))

    @pl.loop(0, gather_steps + 1)
    def _(step):
        @pl.when(step == word_step)
        def _():
            @pl.when(z + NEAR <= top)
            def _():
                pl.semaphore_wait(word, 1)

            @pl.when(z >= NEAR)
            def _():
                pl.semaphore_signal(word, 1, device_id=chip(z - NEAR), device_id_type=MESH)

        @pl.loop(0, 3)
        def _(source):
            each_passed_on(source, step, True, lambda copy: copy.start())
            owner, comes = gathered(source, step - 1)

            @pl.when(comes)
            def _():
                sibling_copy(owner, 1 - core).wait_recv()
                one(zo=owner, diagonal=False)

    inv_mass = 1.0 / stats[1:2, :]
    stats[2:3, :] = stats[2:3, :] * inv_mass
    stats[1:2, :] = inv_mass
    dq_t[...] = jnp.zeros_like(dq_t)

    order = [d for d in SCATTER_ORDER if d <= reach]
    down_table = {i: d for i, d in enumerate(order)}
    down_table[reach] = 0
    down_parent, wrap_parent = parents(SCATTER, reach), parents(WRAP, far)
    wrap_slot = {c: i for cs in WRAP.values() for i, c in enumerate(cs)}

    def owed(direction, step):
        distance = pick(step, down_table)
        down = z - distance
        around = step if WRAP_UP else z - reach - 1 - step
        owner = jnp.where(direction == 0, down, around)
        limit = jnp.where(direction == 0, distance >= 0, jnp.logical_and(step >= 0, step < z - reach))
        return owner, jnp.logical_and(owner >= 0, limit)

    def swap(owner):
        return pltpu.make_async_remote_copy(
            swap_out.at[owner], swap_in.at[owner], swap_send.at[owner], swap_recv.at[owner],
            device_id={"ctx": sibling}, device_id_type=MESH,
        )

    def down_copy(distance, part, to):
        return pltpu.make_async_remote_copy(
            down_out.at[distance, part], down_in.at[distance, part],
            down_send.at[distance, part], down_recv.at[distance, part],
            device_id=chip(to), device_id_type=MESH,
        )

    def wrap_copy(owner, slot, part, to):
        return pltpu.make_async_remote_copy(
            wrap_out.at[owner, part], wrap_in.at[owner, slot, part],
            wrap_send.at[owner, part], wrap_recv.at[owner, slot, part],
            device_id=chip(to), device_id_type=MESH,
        )

    def add_swapped(step, direction, owner):
        swap(owner).wait_recv()
        for part in range(2):
            keep[step, direction, part, core] += swap_in[owner, part].astype(F32)

    def add_down(step, distance, part):
        for slot in range(2):
            child = pick(distance, children(SCATTER, reach, slot))

            @pl.when(jnp.logical_and(child > 0, z + child - distance <= top))
            def _():
                down_copy(child, part, z).wait_recv()
                keep[step, 0, part, core] += down_in[child, part].astype(F32)

    def add_wrap(step, owner, part):
        for slot in range(3):
            child = pick(below_top, children(WRAP, far, slot))

            @pl.when(jnp.logical_and(child > 0, owner <= far - child))
            def _():
                wrap_copy(owner, slot, part, z).wait_recv()
                keep[step, 1, part, core] += wrap_in[owner, slot, part].astype(F32)

    def down_target(distance):
        return z - distance + pick(distance, down_parent)

    def each_wrap_send(owner, part, act):
        for slot in range(3):
            @pl.when(pick(below_top, wrap_slot) == slot)
            def _():
                act(wrap_copy(owner, slot, part, top - pick(below_top, wrap_parent)))

        @pl.when(below_top == 0)
        def _():
            act(wrap_copy(owner, 0, part, owner))

    def finish_down(step):
        owner, valid = owed(0, step)

        @pl.when(valid)
        def _():
            distance = z - owner
            add_swapped(step, 0, owner)
            for part in range(2):
                add_down(step, distance, part)
                down_out[distance, part] = keep[step, 0, part, core].astype(BF16)
                down_copy(distance, part, down_target(distance)).start()

    heights = {p * chips + e: height(p, e, far) for p in range(far + 1) for e in range(far - p + 1)}
    tallest = max(heights.values())

    def finish_wrap(now):
        @pl.loop(0, tallest + 1)
        def _(tall):
            step = now - WRAP_LAG[0] - WRAP_LAG[1] * tall
            owner, valid = owed(1, step)

            @pl.when(jnp.logical_and(valid, pick(below_top * chips + owner, heights) == tall))
            def _():
                add_swapped(step, 1, owner)
                for part in range(2):
                    add_wrap(step, owner, part)
                    wrap_out[owner, part] = keep[step, 1, part, core].astype(BF16)
                    each_wrap_send(owner, part, lambda copy: copy.start())

    @pl.loop(0, reach + 1)
    def _(step):
        @pl.loop(0, 2)
        def _(direction):
            owner, valid = owed(direction, step)

            @pl.when(valid)
            def _():
                sums = keep.at[step, direction]
                two(sums=sums, zo=owner)
                for part in range(2):
                    swap_out[owner, part] = sums[part, 1 - core].astype(BF16)
                swap(owner).start()

            @pl.when(direction == 0)
            def _():
                finish_wrap(step)

            @pl.when(direction == 1)
            def _():
                finish_down(step - 1)

    q_part = jnp.zeros((1, HD), F32)
    for h in range(heads):
        cols = slice(h * HD, (h + 1) * HD)
        x = q_raw[:, cols].astype(F32)
        upstream = scale * dq_t[:, cols].T
        grad, part = norm_back(x, inverse_rms(x), q_gain[...], upstream)
        q_part += part
        dq_out[:, cols] = grad.astype(BF16)
    store = pltpu.make_async_copy(dq_out, dq_hbm.at[0], store_sem)
    store.start()

    def offset(i, count):
        away = (i + 1) // 2
        return count // 2 + jnp.where(i % 2 == 1, -away, away)

    def line_copy(i, slot):
        return pltpu.make_async_remote_copy(
            line_out, line_in.at[slot], line_send.at[i], line_recv.at[slot],
            device_id={"ctx": (me + offset(i, n)) % n}, device_id_type=MESH,
        )

    def plane_copy(i, slot):
        return pltpu.make_async_remote_copy(
            plane_out, plane_in.at[slot], plane_send.at[i], plane_recv.at[slot],
            device_id=plane((place + offset(i, group)) % group), device_id_type=MESH,
        )

    line_out[...] = q_part
    line_in[me] = q_part

    @pl.loop(0, n - 1)
    def _(i):
        line_copy(i, me).start()

    @pl.loop(reach + 1, far + 1 + WRAP_LAG[0] + WRAP_LAG[1] * tallest)
    def _(step):
        finish_wrap(step)

    @pl.loop(0, n - 1)
    def _(i):
        line_copy(i, (me + offset(i, n)) % n).wait_recv()

    plane_out[...] = jnp.sum(line_in[...], axis=0)
    plane_in[place] = plane_out[...]

    @pl.loop(0, group - 1)
    def _(i):
        plane_copy(i, place).start()

    add_swapped(reach, 0, z)
    for part in range(2):
        add_down(reach, 0, part)

    @pl.when(z <= far)
    def _():
        for part in range(2):
            wrap_copy(z, 0, part, z).wait_recv()
            keep[reach, 0, part, core] += wrap_in[z, 0, part].astype(F32)

    x = k_raw[...].astype(F32)
    upstream = scale * keep[reach, 0, 0, core]
    grad, _ = norm_back(x, inverse_rms(x), k_gain[...], upstream)
    dk_out[0] = grad.astype(BF16)
    dv_out[0] = keep[reach, 0, 1, core].astype(BF16)

    @pl.loop(0, group - 1)
    def _(i):
        plane_copy(i, (place + offset(i, group)) % group).wait_recv()

    q_total = jnp.sum(plane_in[...], axis=0)
    gains_out[0:1] = q_total
    gains_out[1:2] = q_total * q_gain[...] / k_gain[...]

    def left(copy):
        copy.wait_send()

    each_own_send(left)

    @pl.loop(0, gather_steps)
    def _(step):
        @pl.loop(0, 3)
        def _(source):
            each_passed_on(source, step, False, left)

    @pl.loop(0, reach + 1)
    def _(step):
        owner, valid = owed(0, step)

        @pl.when(valid)
        def _():
            swap(owner).wait_send()

            @pl.when(owner < z)
            def _():
                for part in range(2):
                    down_copy(z - owner, part, down_target(z - owner)).wait_send()

        around, around_valid = owed(1, step)

        @pl.when(around_valid)
        def _():
            swap(around).wait_send()
            for part in range(2):
                each_wrap_send(around, part, left)

    @pl.loop(0, n - 1)
    def _(i):
        line_copy(i, me).wait_send()

    @pl.loop(0, group - 1)
    def _(i):
        plane_copy(i, place).wait_send()

    store.wait()


def hand_over(*refs):
    count = len(refs) // 2
    for i in range(count):
        refs[count + i][...] = refs[i][...]


def solution(mesh):
    n, tp, dp = mesh.shape["ctx"], mesh.shape["tp"], mesh.shape["dp"]
    chips, reach = n // 2, n // 4
    far = chips - reach - 2

    def shards(q_raw, k_raw, values_in, grad_out, q_gain, k_gain):
        rows, width = q_raw.shape[1:]
        flat = rows * width // HD
        whole = pl.BlockSpec(memory_space=pltpu.VMEM)
        anywhere = pl.BlockSpec(memory_space=pl.ANY)
        dma = pltpu.SemaphoreType.DMA
        outs = pl.pallas_call(
            functools.partial(kernel, n, tp, dp),
            out_shape=(
                jax.ShapeDtypeStruct(q_raw.shape, BF16),
                jax.ShapeDtypeStruct(k_raw.shape, BF16),
                jax.ShapeDtypeStruct(k_raw.shape, BF16),
                jax.ShapeDtypeStruct((2, HD), F32),
            ),
            in_specs=[anywhere] * 4 + [whole] * 2,
            out_specs=(anywhere, whole, whole, whole),
            scratch_shapes=[
                pltpu.VMEM((rows, width), BF16),
                pltpu.VMEM((rows, HD), BF16),
                pltpu.VMEM((flat, HD), BF16),
                pltpu.VMEM((flat, HD), BF16),
                pltpu.VMEM((n, 2, HD, HD), BF16),
                pltpu.VMEM((chips, 2 * HD, flat), F32),
                pltpu.VMEM((chips, 2 * HD, flat), F32),
                pltpu.VMEM((chips, 1, flat), F32),
                pltpu.VMEM((8, flat), F32),
                pltpu.VMEM((2 * HD, flat), BF16),
                pltpu.VMEM((2 * HD, flat), BF16),
                pltpu.VMEM((HD, flat), F32),
                pltpu.VMEM((rows, width), BF16),
                pltpu.VMEM((reach + 1, 2, 2, 2, HD, HD), F32),
                pltpu.VMEM((chips, 2, HD, HD), BF16),
                pltpu.VMEM((chips, 2, HD, HD), BF16),
                pltpu.VMEM((reach + 1, 2, HD, HD), BF16),
                pltpu.VMEM((reach + 1, 2, HD, HD), BF16),
                pltpu.VMEM((far + 1, 2, HD, HD), BF16),
                pltpu.VMEM((far + 1, 3, 2, HD, HD), BF16),
                pltpu.VMEM((1, HD), F32),
                pltpu.VMEM((n, 1, HD), F32),
                pltpu.VMEM((1, HD), F32),
                pltpu.VMEM((tp * dp, 1, HD), F32),
                dma((3,)), dma((flat // HD,)), dma, pltpu.SemaphoreType.REGULAR,
                dma((reach + 1, 2)), dma((reach + 1, 2)),
                dma((far + 1, 2, 2)), dma((far + 1, 2)),
                dma((chips,)), dma((chips,)),
                dma((reach + 1, 2)), dma((reach + 1, 2)),
                dma((far + 1, 2)), dma((far + 1, 3, 2)),
                dma((chips,)), dma((chips,)),
                dma((n,)), dma((n,)),
                dma((tp * dp,)), dma((tp * dp,)),
            ],
            compiler_params=pltpu.CompilerParams(
                collective_id=0, has_side_effects=True, vmem_limit_bytes=60 * 1024 * 1024
            ),
            cost_estimate=pl.CostEstimate(
                flops=10 * flat * n * rows * HD, bytes_accessed=6 * rows * width,
                transcendentals=flat * n * rows,
            ),
        )(q_raw, k_raw, values_in, grad_out, q_gain.reshape(1, HD), k_gain.reshape(1, HD))
        return pl.pallas_call(
            hand_over,
            out_shape=tuple(jax.ShapeDtypeStruct(x.shape, x.dtype) for x in outs),
            in_specs=[whole] * len(outs),
            out_specs=(whole,) * len(outs),
        )(*outs)

    spread = P("dp", "ctx", "tp")
    return jax.shard_map(
        shards,
        mesh=mesh,
        in_specs=(spread, spread, spread, spread, P(), P()),
        out_specs=(spread, spread, spread, P()),
        check_vma=False,
    )
```

```python
import functools
import math

import jax
import jax.numpy as jnp
from jax import lax
from jax.experimental import pallas as pl
from jax.experimental.pallas import tpu as pltpu
from jax.sharding import PartitionSpec as P

HD = 128
CW = 256
EPS = 1e-06
MASKED = -1e30
F32 = jnp.float32
BF16 = jnp.bfloat16
MESH = pl.DeviceIdType.MESH

GATHER = {0: (1, 3), 1: (2,), 3: (4, 6), 4: (5,), 6: (7, 8)}
SCATTER = {0: (1, 3), 1: (2,), 3: (4, 6), 4: (5,), 6: (7, 8)}
AROUND = {0: (1, 3), 1: (2,), 3: (4, 6), 4: (5,)}
WRAP = {0: (1, 3), 1: (2,), 3: (4, 5, 6)}
GATHER_ORDER = (1, 3, 2, 4, 6, 5, 7, 8)
SCATTER_ORDER = (8, 7, 5, 2, 6, 4, 1, 3)
AROUND_DELAY = {0: 0, 1: 2, 3: 2, 2: 4, 4: 4, 6: 4, 5: 5}
WRAP_UP = False
WRAP_LAG = (1, 2)
NEAR = 3


def pick(index, table):
    out = jnp.int32(-1)
    for key, value in table.items():
        out = jnp.where(index == key, value, out)
    return out


def children(tree, reach, slot):
    kept = {d: [c for c in cs if c <= reach] for d, cs in tree.items()}
    return {d: cs[slot] for d, cs in kept.items() if len(cs) > slot}


def height(place, owner, far):
    below = [1 + height(c, owner, far) for c in WRAP.get(place, ()) if owner <= far - c]
    return max(below, default=0)


def parents(tree, reach):
    return {c: d for d, cs in tree.items() for c in cs if c <= reach}


def dot(a, b, contract):
    return lax.dot_general(
        a, b, (((contract[0],), (contract[1],)), ((), ())), preferred_element_type=F32
    )


def inverse_rms(x):
    return lax.rsqrt(jnp.mean(x * x, axis=1, keepdims=True) + EPS)


def norm_back(x, inv, gain, upstream):
    scaled = gain * upstream
    inner = jnp.mean(scaled * x, axis=1, keepdims=True)
    grad = inv * scaled - x * (inv * inv * inv) * inner
    return grad, jnp.sum(upstream * x * inv, axis=0, keepdims=True)


def first_pass(kv, qh, go, probs, dprobs, block_max, stats, zo, core, diagonal, scale2):
    keys = kv[pl.ds(2 * zo, 2), 0].reshape(2 * HD, HD)
    vals = kv[pl.ds(2 * zo, 2), 1].reshape(2 * HD, HD)
    total = qh.shape[0]
    for start in range(0, total, CW):
        cols = slice(start, start + CW)
        s = dot(keys, qh[cols, :], (1, 1))
        if diagonal:
            key_pos = lax.broadcasted_iota(jnp.int32, (2 * HD, CW), 0)
            query_pos = core * HD + lax.broadcasted_iota(jnp.int32, (2 * HD, CW), 1) % HD
            s = jnp.where(key_pos <= query_pos, s, MASKED)
        dp = dot(vals, go[cols, :], (1, 1))
        top = jnp.max(s, axis=0, keepdims=True)
        if not diagonal:
            old = stats[0:1, cols]
            top = jnp.maximum(top, old)
        p = jnp.exp2(s * scale2 - top * scale2)
        mass = jnp.sum(p, axis=0, keepdims=True)
        weighted = jnp.sum(p * dp, axis=0, keepdims=True)
        if not diagonal:
            shrink = jnp.exp2((old - top) * scale2)
            mass += stats[1:2, cols] * shrink
            weighted += stats[2:3, cols] * shrink
        stats[0:1, cols] = top
        stats[1:2, cols] = mass
        stats[2:3, cols] = weighted
        block_max[zo, :, cols] = top
        probs[zo, :, cols] = p
        dprobs[zo, :, cols] = dp


def second_pass(kv, qh, go, probs, dprobs, block_max, stats, prob_b, dscore_b, dq_t, sums, zo, scale2):
    total = qh.shape[0]
    keys = kv[pl.ds(2 * zo, 2), 0].reshape(2 * HD, HD)
    for start in range(0, total, CW):
        cols = slice(start, start + CW)
        factor = jnp.exp2((block_max[zo, :, cols] - stats[0:1, cols]) * scale2) * stats[1:2, cols]
        p = probs[zo, :, cols] * factor
        ds = p * (dprobs[zo, :, cols] - stats[2:3, cols])
        prob_b[:, cols] = p.astype(BF16)
        ds = ds.astype(BF16)
        dscore_b[:, cols] = ds
        dq_t[:, cols] += dot(keys, ds, (0, 0))
    sums[0] = dot(dscore_b[...], qh[...], (1, 0)).reshape(2, HD, HD)
    sums[1] = dot(prob_b[...], go[...], (1, 0)).reshape(2, HD, HD)


def kernel(
    n, tp, dp,
    q_hbm, k_hbm, v_hbm, g_hbm, q_gain, k_gain,
    dq_hbm, dk_out, dv_out, gains_out,
    q_raw, k_raw, qh, go, kv, probs, dprobs, block_max, stats, prob_b, dscore_b, dq_t, dq_out,
    keep, swap_out, swap_in, down_out, down_in, wrap_out, wrap_in,
    line_out, line_in, plane_out, plane_in,
    load_sem, head_sem, store_sem, word,
    up_send, up_recv, around_send, around_recv, sib_send, sib_recv,
    down_send, down_recv, wrap_send, wrap_recv, swap_send, swap_recv,
    line_send, line_recv, plane_send, plane_recv,
):
    chips, heads = n // 2, qh.shape[0] // HD
    reach = chips // 2
    far = chips - reach - 2
    top = chips - 1
    scale = HD ** (-0.5)
    scale2 = scale * math.log2(math.e)
    me = lax.axis_index("ctx")
    z, core = me // 2, me % 2
    sibling = me + 1 - 2 * core
    place = lax.axis_index("tp") * dp + lax.axis_index("dp")
    group = tp * dp
    below_top = top - z

    def chip(to):
        return {"ctx": 2 * to + core}

    def plane(to):
        return {"tp": to // dp, "dp": to % dp}

    barrier = pltpu.get_barrier_semaphore()

    def greet(to):
        pl.semaphore_signal(barrier, 1, device_id=chip(to), device_id_type=MESH)

    greeted = jnp.int32(group)
    for away in range(1, NEAR + 1):
        for to in (z + away, z - away):
            inside = jnp.logical_and(to >= 0, to <= top)
            greeted += jnp.where(inside, 1, 0)

            @pl.when(inside)
            def _():
                greet(to)

    greeted += jnp.where(z <= far, 1, 0)

    @pl.when(z == top)
    def _():
        @pl.loop(0, far + 1)
        def _(i):
            greet(i)

    pl.semaphore_signal(barrier, 1, device_id={"ctx": sibling}, device_id_type=MESH)

    @pl.loop(1, group)
    def _(i):
        pl.semaphore_signal(barrier, 1, device_id=plane((place + i) % group), device_id_type=MESH)

    def load(i):
        src, dst = ((k_hbm.at[0], k_raw), (v_hbm.at[0], kv.at[me, 1]), (q_hbm.at[0], q_raw))[i]
        return pltpu.make_async_copy(src, dst, load_sem.at[i])

    def load_head(h):
        return pltpu.make_async_copy(
            g_hbm.at[0, :, pl.ds(h * HD, HD)], go.at[pl.ds(h * HD, HD)], head_sem.at[h]
        )

    for i in range(3):
        load(i).start()
    for h in range(heads):
        load_head(h).start()

    load(0).wait()
    x = k_raw[...].astype(F32)
    kv[me, 0] = (x * inverse_rms(x) * k_gain[...]).astype(BF16)
    load(1).wait()

    def up_copy(owner, distance, part, to):
        block = kv.at[2 * owner + core, part]
        return pltpu.make_async_remote_copy(
            block, block, up_send.at[distance, part], up_recv.at[distance, part],
            device_id=chip(to), device_id_type=MESH,
        )

    def around_copy(owner, slot, part, to):
        block = kv.at[2 * owner + core, part]
        return pltpu.make_async_remote_copy(
            block, block, around_send.at[owner, slot, part], around_recv.at[owner, part],
            device_id=chip(to), device_id_type=MESH,
        )

    def sibling_copy(owner, owner_core):
        block = kv.at[2 * owner + owner_core]
        return pltpu.make_async_remote_copy(
            block, block, sib_send.at[owner], sib_recv.at[owner],
            device_id={"ctx": sibling}, device_id_type=MESH,
        )

    def each_up_send(distance, part, act):
        for slot in (1, 0):
            child = pick(distance, children(GATHER, reach, slot))
            to = z + child - distance

            @pl.when(jnp.logical_and(child > 0, to <= top))
            def _():
                act(up_copy(z - distance, child, part, to))

    def each_around_send(owner, part, act):
        for slot in (1, 0):
            child = pick(below_top, children(AROUND, far, slot))

            @pl.when(jnp.logical_and(child > 0, owner <= far - child))
            def _():
                act(around_copy(owner, slot, part, top - child))

    def each_own_send(act):
        for part in range(2):
            @pl.when(z <= far)
            def _():
                act(around_copy(z, 0, part, top))

            each_up_send(0, part, act)

        act(sibling_copy(z, core))

    pl.semaphore_wait(barrier, greeted)
    each_own_send(lambda copy: copy.start())

    load(2).wait()
    for h in range(heads):
        cols = slice(h * HD, (h + 1) * HD)
        x = q_raw[:, cols].astype(F32)
        qh[cols, :] = (x * inverse_rms(x) * q_gain[...]).astype(BF16)
    for h in range(heads):
        load_head(h).wait()

    one = functools.partial(
        first_pass, kv, qh, go, probs, dprobs, block_max, stats, core=core, scale2=scale2
    )
    two = functools.partial(
        second_pass, kv, qh, go, probs, dprobs, block_max, stats, prob_b, dscore_b, dq_t, scale2=scale2
    )

    sibling_copy(z, 1 - core).wait_recv()
    one(zo=z, diagonal=True)

    up_table = {i: d for i, d in enumerate(d for d in GATHER_ORDER if d <= reach)}
    delay = pick(below_top, AROUND_DELAY)
    gather_steps = max(reach, 1 + max((far - d) // 2 + late for d, late in AROUND_DELAY.items() if d <= far))
    word_step = jnp.minimum(2 * (below_top // NEAR), gather_steps)

    def gathered(source, step):
        distance = pick(step, up_table)
        up = z - distance
        around = 2 * (step - delay) + source - 1
        up_valid = jnp.logical_and(distance > 0, up >= 0)
        around_valid = jnp.logical_and(
            below_top <= far, jnp.logical_and(step >= delay, around <= far - below_top)
        )
        owner = jnp.where(source == 0, up, around)
        return owner, jnp.logical_or(
            jnp.logical_and(source == 0, up_valid), jnp.logical_and(source >= 1, around_valid)
        )

    def each_passed_on(source, step, arrival, act):
        owner, comes = gathered(source, step)

        @pl.when(jnp.logical_and(comes, source == 0))
        def _():
            for part in range(2):
                if arrival:
                    up_copy(owner, z - owner, part, z).wait_recv()
                each_up_send(z - owner, part, act)

        @pl.when(jnp.logical_and(comes, source >= 1))
        def _():
            for part in range(2):
                if arrival:
                    around_copy(owner, 0, part, z).wait_recv()
                each_around_send(owner, part, act)

        @pl.when(comes)
        def _():
            act(sibling_copy(owner, core))

    @pl.loop(0, gather_steps + 1)
    def _(step):
        @pl.when(step == word_step)
        def _():
            @pl.when(z + NEAR <= top)
            def _():
                pl.semaphore_wait(word, 1)

            @pl.when(z >= NEAR)
            def _():
                pl.semaphore_signal(word, 1, device_id=chip(z - NEAR), device_id_type=MESH)

        @pl.loop(0, 3)
        def _(source):
            each_passed_on(source, step, True, lambda copy: copy.start())
            owner, comes = gathered(source, step - 1)

            @pl.when(comes)
            def _():
                sibling_copy(owner, 1 - core).wait_recv()
                one(zo=owner, diagonal=False)

    inv_mass = 1.0 / stats[1:2, :]
    stats[2:3, :] = stats[2:3, :] * inv_mass
    stats[1:2, :] = inv_mass
    dq_t[...] = jnp.zeros_like(dq_t)

    order = [d for d in SCATTER_ORDER if d <= reach]
    down_table = {i: d for i, d in enumerate(order)}
    down_table[reach] = 0
    down_parent, wrap_parent = parents(SCATTER, reach), parents(WRAP, far)
    wrap_slot = {c: i for cs in WRAP.values() for i, c in enumerate(cs)}

    def owed(direction, step):
        distance = pick(step, down_table)
        down = z - distance
        around = step if WRAP_UP else z - reach - 1 - step
        owner = jnp.where(direction == 0, down, around)
        limit = jnp.where(direction == 0, distance >= 0, jnp.logical_and(step >= 0, step < z - reach))
        return owner, jnp.logical_and(owner >= 0, limit)

    def swap(owner):
        return pltpu.make_async_remote_copy(
            swap_out.at[owner], swap_in.at[owner], swap_send.at[owner], swap_recv.at[owner],
            device_id={"ctx": sibling}, device_id_type=MESH,
        )

    def down_copy(distance, part, to):
        return pltpu.make_async_remote_copy(
            down_out.at[distance, part], down_in.at[distance, part],
            down_send.at[distance, part], down_recv.at[distance, part],
            device_id=chip(to), device_id_type=MESH,
        )

    def wrap_copy(owner, slot, part, to):
        return pltpu.make_async_remote_copy(
            wrap_out.at[owner, part], wrap_in.at[owner, slot, part],
            wrap_send.at[owner, part], wrap_recv.at[owner, slot, part],
            device_id=chip(to), device_id_type=MESH,
        )

    def add_swapped(step, direction, owner):
        swap(owner).wait_recv()
        for part in range(2):
            keep[step, direction, part, core] += swap_in[owner, part].astype(F32)

    def add_down(step, distance, part):
        for slot in range(2):
            child = pick(distance, children(SCATTER, reach, slot))

            @pl.when(jnp.logical_and(child > 0, z + child - distance <= top))
            def _():
                down_copy(child, part, z).wait_recv()
                keep[step, 0, part, core] += down_in[child, part].astype(F32)

    def add_wrap(step, owner, part):
        for slot in range(3):
            child = pick(below_top, children(WRAP, far, slot))

            @pl.when(jnp.logical_and(child > 0, owner <= far - child))
            def _():
                wrap_copy(owner, slot, part, z).wait_recv()
                keep[step, 1, part, core] += wrap_in[owner, slot, part].astype(F32)

    def down_target(distance):
        return z - distance + pick(distance, down_parent)

    def each_wrap_send(owner, part, act):
        for slot in range(3):
            @pl.when(pick(below_top, wrap_slot) == slot)
            def _():
                act(wrap_copy(owner, slot, part, top - pick(below_top, wrap_parent)))

        @pl.when(below_top == 0)
        def _():
            act(wrap_copy(owner, 0, part, owner))

    def waits_down(distance):
        out = False
        for slot in range(2):
            child = pick(distance, children(SCATTER, reach, slot))
            out = jnp.logical_or(out, jnp.logical_and(child > 0, z + child - distance <= top))
        return out

    def finish_down(step, waiting):
        owner, valid = owed(0, step)
        valid = jnp.logical_and(valid, waits_down(z - owner) == waiting)

        @pl.when(valid)
        def _():
            distance = z - owner
            to = down_target(distance)
            swap(owner).wait_recv()
            for part in range(2):
                if waiting:
                    keep[step, 0, part, core] += swap_in[owner, part].astype(F32)
                    add_down(step, distance, part)
                    down_out[distance, part] = keep[step, 0, part, core].astype(BF16)
                else:
                    both = keep[step, 0, part, core] + swap_in[owner, part].astype(F32)
                    down_out[distance, part] = both.astype(BF16)
                down_copy(distance, part, to).start()

    heights = {p * chips + e: height(p, e, far) for p in range(far + 1) for e in range(far - p + 1)}
    tallest = max(heights.values())

    def finish_wrap(now):
        @pl.loop(0, tallest + 1)
        def _(tall):
            step = now - WRAP_LAG[0] - WRAP_LAG[1] * tall
            owner, valid = owed(1, step)

            @pl.when(jnp.logical_and(valid, pick(below_top * chips + owner, heights) == tall))
            def _():
                add_swapped(step, 1, owner)
                for part in range(2):
                    add_wrap(step, owner, part)
                    wrap_out[owner, part] = keep[step, 1, part, core].astype(BF16)
                    each_wrap_send(owner, part, lambda copy: copy.start())

    @pl.loop(0, reach + 1)
    def _(step):
        @pl.loop(0, 2)
        def _(direction):
            owner, valid = owed(direction, step)

            @pl.when(valid)
            def _():
                sums = keep.at[step, direction]
                two(sums=sums, zo=owner)
                for part in range(2):
                    swap_out[owner, part] = sums[part, 1 - core].astype(BF16)
                swap(owner).start()

            @pl.when(direction == 0)
            def _():
                finish_wrap(step)

            @pl.when(direction == 1)
            def _():
                finish_down(step - 1, False)

    q_part = jnp.zeros((1, HD), F32)
    for h in range(heads):
        cols = slice(h * HD, (h + 1) * HD)
        x = q_raw[:, cols].astype(F32)
        upstream = scale * dq_t[:, cols].T
        grad, part = norm_back(x, inverse_rms(x), q_gain[...], upstream)
        q_part += part
        dq_out[:, cols] = grad.astype(BF16)
    store = pltpu.make_async_copy(dq_out, dq_hbm.at[0], store_sem)
    store.start()

    def offset(i, count):
        away = (i + 1) // 2
        return count // 2 + jnp.where(i % 2 == 1, -away, away)

    def line_copy(i, slot):
        return pltpu.make_async_remote_copy(
            line_out, line_in.at[slot], line_send.at[i], line_recv.at[slot],
            device_id={"ctx": (me + offset(i, n)) % n}, device_id_type=MESH,
        )

    def plane_copy(i, slot):
        return pltpu.make_async_remote_copy(
            plane_out, plane_in.at[slot], plane_send.at[i], plane_recv.at[slot],
            device_id=plane((place + offset(i, group)) % group), device_id_type=MESH,
        )

    line_out[...] = q_part
    line_in[me] = q_part

    @pl.loop(0, n - 1)
    def _(i):
        line_copy(i, me).start()

    last = far + 1 + WRAP_LAG[0] + WRAP_LAG[1] * tallest
    @pl.loop(0, max(reach, last))
    def _(step):
        @pl.when(step < reach)
        def _():
            finish_down(step, True)

        @pl.when(step > reach)
        def _():
            finish_wrap(step)

    @pl.loop(0, n - 1)
    def _(i):
        line_copy(i, (me + offset(i, n)) % n).wait_recv()

    plane_out[...] = jnp.sum(line_in[...], axis=0)
    plane_in[place] = plane_out[...]

    @pl.loop(0, group - 1)
    def _(i):
        plane_copy(i, place).start()

    add_swapped(reach, 0, z)
    for part in range(2):
        add_down(reach, 0, part)

    @pl.when(z <= far)
    def _():
        for part in range(2):
            wrap_copy(z, 0, part, z).wait_recv()
            keep[reach, 0, part, core] += wrap_in[z, 0, part].astype(F32)

    x = k_raw[...].astype(F32)
    upstream = scale * keep[reach, 0, 0, core]
    grad, _ = norm_back(x, inverse_rms(x), k_gain[...], upstream)
    dk_out[0] = grad.astype(BF16)
    dv_out[0] = keep[reach, 0, 1, core].astype(BF16)

    def left(copy):
        copy.wait_send()

    each_own_send(left)

    @pl.loop(0, gather_steps)
    def _(step):
        @pl.loop(0, 3)
        def _(source):
            each_passed_on(source, step, False, left)

    @pl.loop(0, reach + 1)
    def _(step):
        owner, valid = owed(0, step)

        @pl.when(valid)
        def _():
            swap(owner).wait_send()

            @pl.when(owner < z)
            def _():
                for part in range(2):
                    down_copy(z - owner, part, down_target(z - owner)).wait_send()

        around, around_valid = owed(1, step)

        @pl.when(around_valid)
        def _():
            swap(around).wait_send()
            for part in range(2):
                each_wrap_send(around, part, left)

    @pl.loop(0, n - 1)
    def _(i):
        line_copy(i, me).wait_send()

    store.wait()

    @pl.loop(0, group - 1)
    def _(i):
        plane_copy(i, (place + offset(i, group)) % group).wait_recv()

    q_total = jnp.sum(plane_in[...], axis=0)
    gains_out[0:1] = q_total
    gains_out[1:2] = q_total * q_gain[...] / k_gain[...]

    @pl.loop(0, group - 1)
    def _(i):
        plane_copy(i, place).wait_send()


def hand_over(*refs):
    count = len(refs) // 2
    for i in range(count):
        refs[count + i][...] = refs[i][...]


def solution(mesh):
    n, tp, dp = mesh.shape["ctx"], mesh.shape["tp"], mesh.shape["dp"]
    chips, reach = n // 2, n // 4
    far = chips - reach - 2

    def shards(q_raw, k_raw, values_in, grad_out, q_gain, k_gain):
        rows, width = q_raw.shape[1:]
        flat = rows * width // HD
        whole = pl.BlockSpec(memory_space=pltpu.VMEM)
        anywhere = pl.BlockSpec(memory_space=pl.ANY)
        dma = pltpu.SemaphoreType.DMA
        outs = pl.pallas_call(
            functools.partial(kernel, n, tp, dp),
            out_shape=(
                jax.ShapeDtypeStruct(q_raw.shape, BF16),
                jax.ShapeDtypeStruct(k_raw.shape, BF16),
                jax.ShapeDtypeStruct(k_raw.shape, BF16),
                jax.ShapeDtypeStruct((2, HD), F32),
            ),
            in_specs=[anywhere] * 4 + [whole] * 2,
            out_specs=(anywhere, whole, whole, whole),
            scratch_shapes=[
                pltpu.VMEM((rows, width), BF16),
                pltpu.VMEM((rows, HD), BF16),
                pltpu.VMEM((flat, HD), BF16),
                pltpu.VMEM((flat, HD), BF16),
                pltpu.VMEM((n, 2, HD, HD), BF16),
                pltpu.VMEM((chips, 2 * HD, flat), F32),
                pltpu.VMEM((chips, 2 * HD, flat), F32),
                pltpu.VMEM((chips, 1, flat), F32),
                pltpu.VMEM((8, flat), F32),
                pltpu.VMEM((2 * HD, flat), BF16),
                pltpu.VMEM((2 * HD, flat), BF16),
                pltpu.VMEM((HD, flat), F32),
                pltpu.VMEM((rows, width), BF16),
                pltpu.VMEM((reach + 1, 2, 2, 2, HD, HD), F32),
                pltpu.VMEM((chips, 2, HD, HD), BF16),
                pltpu.VMEM((chips, 2, HD, HD), BF16),
                pltpu.VMEM((reach + 1, 2, HD, HD), BF16),
                pltpu.VMEM((reach + 1, 2, HD, HD), BF16),
                pltpu.VMEM((far + 1, 2, HD, HD), BF16),
                pltpu.VMEM((far + 1, 3, 2, HD, HD), BF16),
                pltpu.VMEM((1, HD), F32),
                pltpu.VMEM((n, 1, HD), F32),
                pltpu.VMEM((1, HD), F32),
                pltpu.VMEM((tp * dp, 1, HD), F32),
                dma((3,)), dma((flat // HD,)), dma, pltpu.SemaphoreType.REGULAR,
                dma((reach + 1, 2)), dma((reach + 1, 2)),
                dma((far + 1, 2, 2)), dma((far + 1, 2)),
                dma((chips,)), dma((chips,)),
                dma((reach + 1, 2)), dma((reach + 1, 2)),
                dma((far + 1, 2)), dma((far + 1, 3, 2)),
                dma((chips,)), dma((chips,)),
                dma((n,)), dma((n,)),
                dma((tp * dp,)), dma((tp * dp,)),
            ],
            compiler_params=pltpu.CompilerParams(
                collective_id=0, has_side_effects=True, vmem_limit_bytes=60 * 1024 * 1024
            ),
            cost_estimate=pl.CostEstimate(
                flops=10 * flat * n * rows * HD, bytes_accessed=6 * rows * width,
                transcendentals=flat * n * rows,
            ),
        )(q_raw, k_raw, values_in, grad_out, q_gain.reshape(1, HD), k_gain.reshape(1, HD))
        return pl.pallas_call(
            hand_over,
            out_shape=tuple(jax.ShapeDtypeStruct(x.shape, x.dtype) for x in outs),
            in_specs=[whole] * len(outs),
            out_specs=(whole,) * len(outs),
        )(*outs)

    spread = P("dp", "ctx", "tp")
    return jax.shard_map(
        shards,
        mesh=mesh,
        in_specs=(spread, spread, spread, spread, P(), P()),
        out_specs=(spread, spread, spread, P()),
        check_vma=False,
    )
```

```python
import functools
import math

import jax
import jax.numpy as jnp
from jax import lax
from jax.experimental import pallas as pl
from jax.experimental.pallas import tpu as pltpu
from jax.sharding import PartitionSpec as P

HD = 128
CW = 512
EPS = 1e-06
MASKED = -1e30
F32 = jnp.float32
BF16 = jnp.bfloat16
MESH = pl.DeviceIdType.MESH

GATHER = {0: (1, 2), 2: (3, 4), 4: (5, 6), 6: (7, 8)}
SCATTER = {0: (1, 3), 1: (2,), 3: (4, 6), 4: (5,), 6: (7, 8)}
AROUND = {0: (1, 3), 1: (2,), 3: (4, 6), 4: (5,)}
WRAP = {0: (1, 3), 1: (2,), 3: (4, 5, 6)}
GATHER_ORDER = (2, 1, 4, 3, 6, 5, 8, 7)
SCATTER_ORDER = (8, 7, 5, 2, 6, 4, 1, 3)
AROUND_DELAY = {0: 0, 1: 2, 3: 2, 2: 4, 4: 4, 6: 4, 5: 5}
WRAP_UP = False
WRAP_LAG = (1, 2)
NEAR = 3


def pick(index, table):
    out = jnp.int32(-1)
    for key, value in table.items():
        out = jnp.where(index == key, value, out)
    return out


def around_ring(index, size):
    return jnp.where(index >= size, index - size, index)


def children(tree, reach, slot):
    kept = {d: [c for c in cs if c <= reach] for d, cs in tree.items()}
    return {d: cs[slot] for d, cs in kept.items() if len(cs) > slot}


def height(place, owner, far):
    below = [1 + height(c, owner, far) for c in WRAP.get(place, ()) if owner <= far - c]
    return max(below, default=0)


def parents(tree, reach):
    return {c: d for d, cs in tree.items() for c in cs if c <= reach}


def dot(a, b, contract):
    return lax.dot_general(
        a, b, (((contract[0],), (contract[1],)), ((), ())), preferred_element_type=F32
    )


def inverse_rms(x):
    return lax.rsqrt(jnp.mean(x * x, axis=1, keepdims=True) + EPS)


def norm_back(x, inv, gain, upstream):
    scaled = gain * upstream
    inner = jnp.mean(scaled * x, axis=1, keepdims=True)
    grad = inv * scaled - x * (inv * inv * inv) * inner
    return grad, jnp.sum(upstream * x * inv, axis=0, keepdims=True)


def first_pass(kv, qh, go, probs, dprobs, block_max, stats, zo, core, diagonal, scale2):
    keys = kv[pl.ds(2 * zo, 2), 0].reshape(2 * HD, HD)
    vals = kv[pl.ds(2 * zo, 2), 1].reshape(2 * HD, HD)
    total = qh.shape[0]
    for start in range(0, total, CW):
        cols = slice(start, start + CW)
        s = dot(keys, qh[cols, :], (1, 1))
        if diagonal:
            key_pos = lax.broadcasted_iota(jnp.int32, (2 * HD, CW), 0)
            query_pos = core * HD + lax.broadcasted_iota(jnp.int32, (2 * HD, CW), 1) % HD
            s = jnp.where(key_pos <= query_pos, s, MASKED)
        dp = dot(vals, go[cols, :], (1, 1))
        top = jnp.max(s, axis=0, keepdims=True)
        if not diagonal:
            old = stats[0:1, cols]
            top = jnp.maximum(top, old)
        p = jnp.exp2(s * scale2 - top * scale2)
        mass = jnp.sum(p, axis=0, keepdims=True)
        weighted = jnp.sum(p * dp, axis=0, keepdims=True)
        if not diagonal:
            shrink = jnp.exp2((old - top) * scale2)
            mass += stats[1:2, cols] * shrink
            weighted += stats[2:3, cols] * shrink
        stats[0:1, cols] = top
        stats[1:2, cols] = mass
        stats[2:3, cols] = weighted
        block_max[zo, :, cols] = top
        probs[zo, :, cols] = p
        dprobs[zo, :, cols] = dp


def second_pass(kv, qh, go, probs, dprobs, block_max, stats, prob_b, dscore_b, dq_t, sums, zo, scale2):
    total = qh.shape[0]
    keys = kv[pl.ds(2 * zo, 2), 0].reshape(2 * HD, HD)
    for start in range(0, total, CW):
        cols = slice(start, start + CW)
        factor = jnp.exp2((block_max[zo, :, cols] - stats[0:1, cols]) * scale2) * stats[1:2, cols]
        p = probs[zo, :, cols] * factor
        ds = p * (dprobs[zo, :, cols] - stats[2:3, cols])
        prob_b[:, cols] = p.astype(BF16)
        ds = ds.astype(BF16)
        dscore_b[:, cols] = ds
        dq_t[:, cols] += dot(keys, ds, (0, 0))
    sums[0] = dot(dscore_b[...], qh[...], (1, 0)).reshape(2, HD, HD)
    sums[1] = dot(prob_b[...], go[...], (1, 0)).reshape(2, HD, HD)


def kernel(
    n, tp, dp,
    q_hbm, k_hbm, v_hbm, g_hbm, q_gain, k_gain,
    dq_hbm, dk_out, dv_out, gains_out,
    q_raw, k_raw, qh, go, kv, probs, dprobs, block_max, stats, prob_b, dscore_b, dq_t, dq_out,
    keep, swap_out, swap_in, down_out, down_in, wrap_out, wrap_in,
    line_out, line_in, plane_out, plane_in,
    load_sem, head_sem, store_sem, word,
    up_send, up_recv, around_send, around_recv, sib_send, sib_recv,
    down_send, down_recv, wrap_send, wrap_recv, swap_send, swap_recv,
    line_send, line_recv, plane_send, plane_recv,
):
    chips, heads = n // 2, qh.shape[0] // HD
    reach = chips // 2
    far = chips - reach - 2
    top = chips - 1
    scale = HD ** (-0.5)
    scale2 = scale * math.log2(math.e)
    me = lax.axis_index("ctx")
    z, core = me // 2, me % 2
    sibling = me + 1 - 2 * core
    place = lax.axis_index("tp") * dp + lax.axis_index("dp")
    group = tp * dp
    below_top = top - z

    def chip(to):
        return {"ctx": 2 * to + core}

    def plane(to):
        return {"tp": to // dp, "dp": to % dp}

    barrier = pltpu.get_barrier_semaphore()

    def greet(to):
        pl.semaphore_signal(barrier, 1, device_id=chip(to), device_id_type=MESH)

    greeted = jnp.int32(group)
    for away in range(1, NEAR + 1):
        for to in (z + away, z - away):
            inside = jnp.logical_and(to >= 0, to <= top)
            greeted += jnp.where(inside, 1, 0)

            @pl.when(inside)
            def _():
                greet(to)

    greeted += jnp.where(z <= far, 1, 0)

    @pl.when(z == top)
    def _():
        @pl.loop(0, far + 1)
        def _(i):
            greet(i)

    pl.semaphore_signal(barrier, 1, device_id={"ctx": sibling}, device_id_type=MESH)

    @pl.loop(1, group)
    def _(i):
        pl.semaphore_signal(barrier, 1, device_id=plane((place + i) % group), device_id_type=MESH)

    def load(i):
        src, dst = ((k_hbm.at[0], k_raw), (v_hbm.at[0], kv.at[me, 1]), (q_hbm.at[0], q_raw))[i]
        return pltpu.make_async_copy(src, dst, load_sem.at[i])

    def load_head(h):
        return pltpu.make_async_copy(
            g_hbm.at[0, :, pl.ds(h * HD, HD)], go.at[pl.ds(h * HD, HD)], head_sem.at[h]
        )

    for i in range(3):
        load(i).start()
    for h in range(heads):
        load_head(h).start()

    load(0).wait()
    x = k_raw[...].astype(F32)
    kv[me, 0] = (x * inverse_rms(x) * k_gain[...]).astype(BF16)
    load(1).wait()

    def up_copy(owner, distance, part, to):
        block = kv.at[2 * owner + core, part]
        return pltpu.make_async_remote_copy(
            block, block, up_send.at[distance, part], up_recv.at[distance, part],
            device_id=chip(to), device_id_type=MESH,
        )

    def around_copy(owner, slot, part, to):
        block = kv.at[2 * owner + core, part]
        return pltpu.make_async_remote_copy(
            block, block, around_send.at[owner, slot, part], around_recv.at[owner, part],
            device_id=chip(to), device_id_type=MESH,
        )

    def sibling_copy(owner, owner_core):
        block = kv.at[2 * owner + owner_core]
        return pltpu.make_async_remote_copy(
            block, block, sib_send.at[owner], sib_recv.at[owner],
            device_id={"ctx": sibling}, device_id_type=MESH,
        )

    def each_up_send(distance, part, act):
        for slot in (1, 0):
            child = pick(distance, children(GATHER, reach, slot))
            to = z + child - distance

            @pl.when(jnp.logical_and(child > 0, to <= top))
            def _():
                act(up_copy(z - distance, child, part, to))

    around_children = [pick(below_top, children(AROUND, far, slot)) for slot in range(2)]

    def each_around_send(owner, part, act):
        for slot in (1, 0):
            child = around_children[slot]

            @pl.when(jnp.logical_and(child > 0, owner <= far - child))
            def _():
                act(around_copy(owner, slot, part, top - child))

    def each_own_send(act):
        for part in range(2):
            @pl.when(z <= far)
            def _():
                act(around_copy(z, 0, part, top))

            each_up_send(0, part, act)

        act(sibling_copy(z, core))

    pl.semaphore_wait(barrier, greeted)
    each_own_send(lambda copy: copy.start())

    load(2).wait()
    for h in range(heads):
        cols = slice(h * HD, (h + 1) * HD)
        x = q_raw[:, cols].astype(F32)
        qh[cols, :] = (x * inverse_rms(x) * q_gain[...]).astype(BF16)
    for h in range(heads):
        load_head(h).wait()

    one = functools.partial(
        first_pass, kv, qh, go, probs, dprobs, block_max, stats, core=core, scale2=scale2
    )
    two = functools.partial(
        second_pass, kv, qh, go, probs, dprobs, block_max, stats, prob_b, dscore_b, dq_t, scale2=scale2
    )

    sibling_copy(z, 1 - core).wait_recv()
    one(zo=z, diagonal=True)

    up_table = {i: d for i, d in enumerate(d for d in GATHER_ORDER if d <= reach)}
    delay = pick(below_top, AROUND_DELAY)
    gather_steps = max(reach, 1 + max((far - d) // 2 + late for d, late in AROUND_DELAY.items() if d <= far))
    word_step = jnp.minimum(2 * (below_top // NEAR), gather_steps)

    def gathered(source, step):
        distance = pick(step, up_table)
        up = z - distance
        around = 2 * (step - delay) + source - 1
        up_valid = jnp.logical_and(distance > 0, up >= 0)
        around_valid = jnp.logical_and(
            below_top <= far, jnp.logical_and(step >= delay, around <= far - below_top)
        )
        owner = jnp.where(source == 0, up, around)
        return owner, jnp.logical_or(
            jnp.logical_and(source == 0, up_valid), jnp.logical_and(source >= 1, around_valid)
        )

    def each_passed_on(source, step, arrival, act):
        owner, comes = gathered(source, step)

        @pl.when(jnp.logical_and(comes, source == 0))
        def _():
            for part in range(2):
                if arrival:
                    up_copy(owner, z - owner, part, z).wait_recv()
                each_up_send(z - owner, part, act)

        @pl.when(jnp.logical_and(comes, source >= 1))
        def _():
            for part in range(2):
                if arrival:
                    around_copy(owner, 0, part, z).wait_recv()
                each_around_send(owner, part, act)

        @pl.when(comes)
        def _():
            act(sibling_copy(owner, core))

    @pl.loop(0, gather_steps + 1)
    def _(step):
        @pl.when(step == word_step)
        def _():
            @pl.when(z + NEAR <= top)
            def _():
                pl.semaphore_wait(word, 1)

            @pl.when(z >= NEAR)
            def _():
                pl.semaphore_signal(word, 1, device_id=chip(z - NEAR), device_id_type=MESH)

        @pl.loop(0, 3)
        def _(source):
            each_passed_on(source, step, True, lambda copy: copy.start())
            owner, comes = gathered(source, step - 1)

            @pl.when(comes)
            def _():
                sibling_copy(owner, 1 - core).wait_recv()
                one(zo=owner, diagonal=False)

    inv_mass = 1.0 / stats[1:2, :]
    stats[2:3, :] = stats[2:3, :] * inv_mass
    stats[1:2, :] = inv_mass
    dq_t[...] = jnp.zeros_like(dq_t)

    order = [d for d in SCATTER_ORDER if d <= reach]
    down_table = {i: d for i, d in enumerate(order)}
    down_table[reach] = 0
    down_parent, wrap_parent = parents(SCATTER, reach), parents(WRAP, far)
    wrap_slot = {c: i for cs in WRAP.values() for i, c in enumerate(cs)}

    def owed(direction, step):
        distance = pick(step, down_table)
        down = z - distance
        around = step if WRAP_UP else z - reach - 1 - step
        owner = jnp.where(direction == 0, down, around)
        limit = jnp.where(direction == 0, distance >= 0, jnp.logical_and(step >= 0, step < z - reach))
        return owner, jnp.logical_and(owner >= 0, limit)

    def swap(owner):
        return pltpu.make_async_remote_copy(
            swap_out.at[owner], swap_in.at[owner], swap_send.at[owner], swap_recv.at[owner],
            device_id={"ctx": sibling}, device_id_type=MESH,
        )

    def down_copy(distance, part, to):
        return pltpu.make_async_remote_copy(
            down_out.at[distance, part], down_in.at[distance, part],
            down_send.at[distance, part], down_recv.at[distance, part],
            device_id=chip(to), device_id_type=MESH,
        )

    def wrap_copy(owner, slot, part, to):
        return pltpu.make_async_remote_copy(
            wrap_out.at[owner, part], wrap_in.at[owner, slot, part],
            wrap_send.at[owner, part], wrap_recv.at[owner, slot, part],
            device_id=chip(to), device_id_type=MESH,
        )

    def add_swapped(step, direction, owner):
        swap(owner).wait_recv()
        for part in range(2):
            keep[step, direction, part, core] += swap_in[owner, part].astype(F32)

    def add_down(step, distance, part):
        for slot in range(2):
            child = pick(distance, children(SCATTER, reach, slot))

            @pl.when(jnp.logical_and(child > 0, z + child - distance <= top))
            def _():
                down_copy(child, part, z).wait_recv()
                keep[step, 0, part, core] += down_in[child, part].astype(F32)

    wrap_children = [pick(below_top, children(WRAP, far, slot)) for slot in range(3)]
    my_slot, my_parent = pick(below_top, wrap_slot), pick(below_top, wrap_parent)

    def add_wrap(step, owner, part):
        for slot in range(3):
            child = wrap_children[slot]

            @pl.when(jnp.logical_and(child > 0, owner <= far - child))
            def _():
                wrap_copy(owner, slot, part, z).wait_recv()
                keep[step, 1, part, core] += wrap_in[owner, slot, part].astype(F32)

    def down_target(distance):
        return z - distance + pick(distance, down_parent)

    def each_wrap_send(owner, part, act):
        for slot in range(3):
            @pl.when(my_slot == slot)
            def _():
                act(wrap_copy(owner, slot, part, top - my_parent))

        @pl.when(below_top == 0)
        def _():
            act(wrap_copy(owner, 0, part, owner))

    def waits_down(distance):
        out = False
        for slot in range(2):
            child = pick(distance, children(SCATTER, reach, slot))
            out = jnp.logical_or(out, jnp.logical_and(child > 0, z + child - distance <= top))
        return out

    def finish_down(step, waiting):
        owner, valid = owed(0, step)
        valid = jnp.logical_and(valid, waits_down(z - owner) == waiting)

        @pl.when(valid)
        def _():
            distance = z - owner
            to = down_target(distance)
            swap(owner).wait_recv()
            for part in range(2):
                if waiting:
                    keep[step, 0, part, core] += swap_in[owner, part].astype(F32)
                    add_down(step, distance, part)
                    down_out[distance, part] = keep[step, 0, part, core].astype(BF16)
                else:
                    both = keep[step, 0, part, core] + swap_in[owner, part].astype(F32)
                    down_out[distance, part] = both.astype(BF16)
                down_copy(distance, part, to).start()

    heights = {(p, e): height(p, e, far) for p in range(far + 1) for e in range(far - p + 1)}
    tallest = max(heights.values())
    limits = []
    for least in range(1, tallest + 1):
        waits = {p: max((e for (q, e), h in heights.items() if q == p and h >= least), default=-1) for p, _ in heights}
        limits.append(pick(below_top, {p: e for p, e in waits.items() if e >= 0}))

    def finish_wrap(now):
        @pl.loop(0, tallest + 1)
        def _(tall):
            step = now - WRAP_LAG[0] - WRAP_LAG[1] * tall
            owner, valid = owed(1, step)

            waits = jnp.int32(0)
            for limit in limits:
                waits += jnp.where(owner <= limit, 1, 0)

            @pl.when(jnp.logical_and(valid, waits == tall))
            def _():
                add_swapped(step, 1, owner)
                for part in range(2):
                    add_wrap(step, owner, part)
                    wrap_out[owner, part] = keep[step, 1, part, core].astype(BF16)
                    each_wrap_send(owner, part, lambda copy: copy.start())

    @pl.loop(0, reach + 1)
    def _(step):
        @pl.loop(0, 2)
        def _(direction):
            owner, valid = owed(direction, step)

            @pl.when(valid)
            def _():
                sums = keep.at[step, direction]
                two(sums=sums, zo=owner)
                for part in range(2):
                    swap_out[owner, part] = sums[part, 1 - core].astype(BF16)
                swap(owner).start()

            @pl.when(direction == 0)
            def _():
                finish_wrap(step)

            @pl.when(direction == 1)
            def _():
                finish_down(step - 1, False)

    q_part = jnp.zeros((1, HD), F32)
    for h in range(heads):
        cols = slice(h * HD, (h + 1) * HD)
        x = q_raw[:, cols].astype(F32)
        upstream = scale * dq_t[:, cols].T
        grad, part = norm_back(x, inverse_rms(x), q_gain[...], upstream)
        q_part += part
        dq_out[:, cols] = grad.astype(BF16)
    store = pltpu.make_async_copy(dq_out, dq_hbm.at[0], store_sem)
    store.start()

    def offset(i, count):
        away = (i + 1) // 2
        return count // 2 + jnp.where(i % 2 == 1, -away, away)

    def line_copy(i, slot):
        return pltpu.make_async_remote_copy(
            line_out, line_in.at[slot], line_send.at[i], line_recv.at[slot],
            device_id={"ctx": around_ring(me + offset(i, n), n)}, device_id_type=MESH,
        )

    def plane_copy(i, slot):
        return pltpu.make_async_remote_copy(
            plane_out, plane_in.at[slot], plane_send.at[i], plane_recv.at[slot],
            device_id=plane(around_ring(place + offset(i, group), group)), device_id_type=MESH,
        )

    line_out[...] = q_part
    line_in[me] = q_part

    @pl.loop(0, n - 1)
    def _(i):
        line_copy(i, me).start()

    last = far + 1 + WRAP_LAG[0] + WRAP_LAG[1] * tallest
    @pl.loop(0, max(reach, last))
    def _(step):
        @pl.when(step < reach)
        def _():
            finish_down(step, True)

        @pl.when(step > reach)
        def _():
            finish_wrap(step)

    @pl.loop(0, n - 1)
    def _(i):
        line_copy(i, around_ring(me + offset(i, n), n)).wait_recv()

    plane_out[...] = jnp.sum(line_in[...], axis=0)
    plane_in[place] = plane_out[...]

    @pl.loop(0, group - 1)
    def _(i):
        plane_copy(i, place).start()

    add_swapped(reach, 0, z)
    for part in range(2):
        add_down(reach, 0, part)

    @pl.when(z <= far)
    def _():
        for part in range(2):
            wrap_copy(z, 0, part, z).wait_recv()
            keep[reach, 0, part, core] += wrap_in[z, 0, part].astype(F32)

    x = k_raw[...].astype(F32)
    upstream = scale * keep[reach, 0, 0, core]
    grad, _ = norm_back(x, inverse_rms(x), k_gain[...], upstream)
    dk_out[0] = grad.astype(BF16)
    dv_out[0] = keep[reach, 0, 1, core].astype(BF16)

    def left(copy):
        copy.wait_send()

    each_own_send(left)

    @pl.loop(0, gather_steps)
    def _(step):
        @pl.loop(0, 3)
        def _(source):
            each_passed_on(source, step, False, left)

    @pl.loop(0, reach + 1)
    def _(step):
        owner, valid = owed(0, step)

        @pl.when(valid)
        def _():
            swap(owner).wait_send()

            @pl.when(owner < z)
            def _():
                for part in range(2):
                    down_copy(z - owner, part, down_target(z - owner)).wait_send()

        around, around_valid = owed(1, step)

        @pl.when(around_valid)
        def _():
            swap(around).wait_send()
            for part in range(2):
                each_wrap_send(around, part, left)

    @pl.loop(0, n - 1)
    def _(i):
        line_copy(i, me).wait_send()

    store.wait()

    @pl.loop(0, group - 1)
    def _(i):
        plane_copy(i, around_ring(place + offset(i, group), group)).wait_recv()

    q_total = jnp.sum(plane_in[...], axis=0)
    gains_out[0:1] = q_total
    gains_out[1:2] = q_total * q_gain[...] / k_gain[...]

    @pl.loop(0, group - 1)
    def _(i):
        plane_copy(i, place).wait_send()


def hand_over(*refs):
    count = len(refs) // 2
    for i in range(count):
        refs[count + i][...] = refs[i][...]


def solution(mesh):
    n, tp, dp = mesh.shape["ctx"], mesh.shape["tp"], mesh.shape["dp"]
    chips, reach = n // 2, n // 4
    far = chips - reach - 2

    def shards(q_raw, k_raw, values_in, grad_out, q_gain, k_gain):
        rows, width = q_raw.shape[1:]
        flat = rows * width // HD
        whole = pl.BlockSpec(memory_space=pltpu.VMEM)
        anywhere = pl.BlockSpec(memory_space=pl.ANY)
        dma = pltpu.SemaphoreType.DMA
        outs = pl.pallas_call(
            functools.partial(kernel, n, tp, dp),
            out_shape=(
                jax.ShapeDtypeStruct(q_raw.shape, BF16),
                jax.ShapeDtypeStruct(k_raw.shape, BF16),
                jax.ShapeDtypeStruct(k_raw.shape, BF16),
                jax.ShapeDtypeStruct((2, HD), F32),
            ),
            in_specs=[anywhere] * 4 + [whole] * 2,
            out_specs=(anywhere, whole, whole, whole),
            scratch_shapes=[
                pltpu.VMEM((rows, width), BF16),
                pltpu.VMEM((rows, HD), BF16),
                pltpu.VMEM((flat, HD), BF16),
                pltpu.VMEM((flat, HD), BF16),
                pltpu.VMEM((n, 2, HD, HD), BF16),
                pltpu.VMEM((chips, 2 * HD, flat), F32),
                pltpu.VMEM((chips, 2 * HD, flat), F32),
                pltpu.VMEM((chips, 1, flat), F32),
                pltpu.VMEM((8, flat), F32),
                pltpu.VMEM((2 * HD, flat), BF16),
                pltpu.VMEM((2 * HD, flat), BF16),
                pltpu.VMEM((HD, flat), F32),
                pltpu.VMEM((rows, width), BF16),
                pltpu.VMEM((reach + 1, 2, 2, 2, HD, HD), F32),
                pltpu.VMEM((chips, 2, HD, HD), BF16),
                pltpu.VMEM((chips, 2, HD, HD), BF16),
                pltpu.VMEM((reach + 1, 2, HD, HD), BF16),
                pltpu.VMEM((reach + 1, 2, HD, HD), BF16),
                pltpu.VMEM((far + 1, 2, HD, HD), BF16),
                pltpu.VMEM((far + 1, 3, 2, HD, HD), BF16),
                pltpu.VMEM((1, HD), F32),
                pltpu.VMEM((n, 1, HD), F32),
                pltpu.VMEM((1, HD), F32),
                pltpu.VMEM((tp * dp, 1, HD), F32),
                dma((3,)), dma((flat // HD,)), dma, pltpu.SemaphoreType.REGULAR,
                dma((reach + 1, 2)), dma((reach + 1, 2)),
                dma((far + 1, 2, 2)), dma((far + 1, 2)),
                dma((chips,)), dma((chips,)),
                dma((reach + 1, 2)), dma((reach + 1, 2)),
                dma((far + 1, 2)), dma((far + 1, 3, 2)),
                dma((chips,)), dma((chips,)),
                dma((n,)), dma((n,)),
                dma((tp * dp,)), dma((tp * dp,)),
            ],
            compiler_params=pltpu.CompilerParams(
                collective_id=0, has_side_effects=True, vmem_limit_bytes=60 * 1024 * 1024
            ),
            cost_estimate=pl.CostEstimate(
                flops=10 * flat * n * rows * HD, bytes_accessed=6 * rows * width,
                transcendentals=flat * n * rows,
            ),
        )(q_raw, k_raw, values_in, grad_out, q_gain.reshape(1, HD), k_gain.reshape(1, HD))
        return pl.pallas_call(
            hand_over,
            out_shape=tuple(jax.ShapeDtypeStruct(x.shape, x.dtype) for x in outs),
            in_specs=[whole] * len(outs),
            out_specs=(whole,) * len(outs),
        )(*outs)

    spread = P("dp", "ctx", "tp")
    return jax.shard_map(
        shards,
        mesh=mesh,
        in_specs=(spread, spread, spread, spread, P(), P()),
        out_specs=(spread, spread, spread, P()),
        check_vma=False,
    )
```

```python
import functools
import math

import jax
import jax.numpy as jnp
from jax import lax
from jax.experimental import pallas as pl
from jax.experimental.pallas import tpu as pltpu
from jax.sharding import PartitionSpec as P

HD = 128
CW = 512
EPS = 1e-06
MASKED = -1e30
F32 = jnp.float32
BF16 = jnp.bfloat16
MESH = pl.DeviceIdType.MESH

GATHER = {0: (1, 2), 2: (3, 4), 4: (5, 6), 6: (7, 8)}
SCATTER = {0: (1, 3), 1: (2,), 3: (4, 6), 4: (5,), 6: (7, 8)}
AROUND = {0: (1, 3), 1: (2,), 3: (4, 6), 4: (5,)}
WRAP = {0: (1, 3), 1: (2,), 3: (4, 5, 6)}
GATHER_ORDER = (2, 1, 4, 3, 6, 5, 8, 7)
SCATTER_ORDER = (8, 7, 5, 2, 6, 4, 1, 3)
AROUND_DELAY = {0: 0, 1: 2, 3: 2, 2: 4, 4: 4, 6: 4, 5: 5}
WRAP_UP = False
WRAP_LAG = (1, 2)
NEAR = 3


def pick(index, table):
    out = jnp.int32(-1)
    for key, value in table.items():
        out = jnp.where(index == key, value, out)
    return out


def around_ring(index, size):
    return jnp.where(index >= size, index - size, index)


def children(tree, reach, slot):
    kept = {d: [c for c in cs if c <= reach] for d, cs in tree.items()}
    return {d: cs[slot] for d, cs in kept.items() if len(cs) > slot}


def height(place, owner, far):
    below = [1 + height(c, owner, far) for c in WRAP.get(place, ()) if owner <= far - c]
    return max(below, default=0)


def parents(tree, reach):
    return {c: d for d, cs in tree.items() for c in cs if c <= reach}


def dot(a, b, contract):
    return lax.dot_general(
        a, b, (((contract[0],), (contract[1],)), ((), ())), preferred_element_type=F32
    )


def inverse_rms(x):
    return lax.rsqrt(jnp.mean(x * x, axis=1, keepdims=True) + EPS)


def norm_back(x, inv, gain, upstream):
    scaled = gain * upstream
    inner = jnp.mean(scaled * x, axis=1, keepdims=True)
    grad = inv * scaled - x * (inv * inv * inv) * inner
    return grad, jnp.sum(upstream * x * inv, axis=0, keepdims=True)


def first_pass(kv, qh, go, probs, dprobs, block_max, stats, zo, core, diagonal, scale2):
    keys = kv[pl.ds(2 * zo, 2), 0].reshape(2 * HD, HD)
    vals = kv[pl.ds(2 * zo, 2), 1].reshape(2 * HD, HD)
    total = qh.shape[0]
    for start in range(0, total, CW):
        cols = slice(start, start + CW)
        s = dot(keys, qh[cols, :], (1, 1))
        if diagonal:
            key_pos = lax.broadcasted_iota(jnp.int32, (2 * HD, CW), 0)
            query_pos = core * HD + lax.broadcasted_iota(jnp.int32, (2 * HD, CW), 1) % HD
            s = jnp.where(key_pos <= query_pos, s, MASKED)
        dp = dot(vals, go[cols, :], (1, 1))
        top = jnp.max(s, axis=0, keepdims=True)
        if not diagonal:
            old = stats[0:1, cols]
            top = jnp.maximum(top, old)
        p = jnp.exp2(s * scale2 - top * scale2)
        mass = jnp.sum(p, axis=0, keepdims=True)
        weighted = jnp.sum(p * dp, axis=0, keepdims=True)
        if not diagonal:
            shrink = jnp.exp2((old - top) * scale2)
            mass += stats[1:2, cols] * shrink
            weighted += stats[2:3, cols] * shrink
        stats[0:1, cols] = top
        stats[1:2, cols] = mass
        stats[2:3, cols] = weighted
        block_max[zo, :, cols] = top
        probs[zo, :, cols] = p
        dprobs[zo, :, cols] = dp


def second_pass(kv, qh, go, probs, dprobs, block_max, stats, prob_b, dscore_b, dq_t, sums, zo, scale2):
    total = qh.shape[0]
    keys = kv[pl.ds(2 * zo, 2), 0].reshape(2 * HD, HD)
    for start in range(0, total, CW):
        cols = slice(start, start + CW)
        factor = jnp.exp2((block_max[zo, :, cols] - stats[0:1, cols]) * scale2) * stats[1:2, cols]
        p = probs[zo, :, cols] * factor
        ds = p * (dprobs[zo, :, cols] - stats[2:3, cols])
        prob_b[:, cols] = p.astype(BF16)
        ds = ds.astype(BF16)
        dscore_b[:, cols] = ds
        dq_t[:, cols] += dot(keys, ds, (0, 0))
    sums[0] = dot(dscore_b[...], qh[...], (1, 0)).reshape(2, HD, HD)
    sums[1] = dot(prob_b[...], go[...], (1, 0)).reshape(2, HD, HD)


def kernel(
    n, tp, dp,
    q_hbm, k_hbm, v_hbm, g_hbm, q_gain, k_gain,
    dq_hbm, dk_out, dv_out, gains_out,
    q_raw, k_raw, qh, go, kv, probs, dprobs, block_max, stats, prob_b, dscore_b, dq_t, dq_out,
    keep, swap_out, swap_in, down_out, down_in, wrap_out, wrap_in,
    line_out, line_in, plane_out, plane_in,
    load_sem, head_sem, store_sem, word,
    up_send, up_recv, around_send, around_recv, sib_send, sib_recv,
    down_send, down_recv, wrap_send, wrap_recv, swap_send, swap_recv,
    line_send, line_recv, plane_send, plane_recv,
):
    chips, heads = n // 2, qh.shape[0] // HD
    reach = chips // 2
    far = chips - reach - 2
    top = chips - 1
    scale = HD ** (-0.5)
    scale2 = scale * math.log2(math.e)
    me = lax.axis_index("ctx")
    z, core = me // 2, me % 2
    sibling = me + 1 - 2 * core
    place = lax.axis_index("tp") * dp + lax.axis_index("dp")
    group = tp * dp
    below_top = top - z

    def chip(to):
        return {"ctx": 2 * to + core}

    def plane(to):
        return {"tp": to // dp, "dp": to % dp}

    barrier = pltpu.get_barrier_semaphore()

    def greet(to):
        pl.semaphore_signal(barrier, 1, device_id=chip(to), device_id_type=MESH)

    greeted = jnp.int32(group)
    for away in range(1, NEAR + 1):
        for to in (z + away, z - away):
            inside = jnp.logical_and(to >= 0, to <= top)
            greeted += jnp.where(inside, 1, 0)

            @pl.when(inside)
            def _():
                greet(to)

    greeted += jnp.where(z <= far, 1, 0)

    @pl.when(z == top)
    def _():
        @pl.loop(0, far + 1)
        def _(i):
            greet(i)

    pl.semaphore_signal(barrier, 1, device_id={"ctx": sibling}, device_id_type=MESH)

    @pl.loop(1, group)
    def _(i):
        pl.semaphore_signal(barrier, 1, device_id=plane((place + i) % group), device_id_type=MESH)

    def load(i):
        src, dst = ((k_hbm.at[0], k_raw), (v_hbm.at[0], kv.at[me, 1]), (q_hbm.at[0], q_raw))[i]
        return pltpu.make_async_copy(src, dst, load_sem.at[i])

    def load_head(h):
        return pltpu.make_async_copy(
            g_hbm.at[0, :, pl.ds(h * HD, HD)], go.at[pl.ds(h * HD, HD)], head_sem.at[h]
        )

    for i in range(3):
        load(i).start()
    for h in range(heads):
        load_head(h).start()

    load(0).wait()
    x = k_raw[...].astype(F32)
    kv[me, 0] = (x * inverse_rms(x) * k_gain[...]).astype(BF16)
    load(1).wait()

    def up_copy(owner, distance, part, to):
        block = kv.at[2 * owner + core, part]
        return pltpu.make_async_remote_copy(
            block, block, up_send.at[distance, part], up_recv.at[distance, part],
            device_id=chip(to), device_id_type=MESH,
        )

    def around_copy(owner, slot, part, to):
        block = kv.at[2 * owner + core, part]
        return pltpu.make_async_remote_copy(
            block, block, around_send.at[owner, slot, part], around_recv.at[owner, part],
            device_id=chip(to), device_id_type=MESH,
        )

    def sibling_copy(owner, owner_core):
        block = kv.at[2 * owner + owner_core]
        return pltpu.make_async_remote_copy(
            block, block, sib_send.at[owner], sib_recv.at[owner],
            device_id={"ctx": sibling}, device_id_type=MESH,
        )

    def each_up_send(distance, part, act):
        for slot in (1, 0):
            child = pick(distance, children(GATHER, reach, slot))
            to = z + child - distance

            @pl.when(jnp.logical_and(child > 0, to <= top))
            def _():
                act(up_copy(z - distance, child, part, to))

    around_children = [pick(below_top, children(AROUND, far, slot)) for slot in range(2)]

    def each_around_send(owner, part, act):
        for slot in (1, 0):
            child = around_children[slot]

            @pl.when(jnp.logical_and(child > 0, owner <= far - child))
            def _():
                act(around_copy(owner, slot, part, top - child))

    def each_own_send(act):
        for part in range(2):
            @pl.when(z <= far)
            def _():
                act(around_copy(z, 0, part, top))

            each_up_send(0, part, act)

        act(sibling_copy(z, core))

    pl.semaphore_wait(barrier, greeted)
    each_own_send(lambda copy: copy.start())

    load(2).wait()
    for h in range(heads):
        cols = slice(h * HD, (h + 1) * HD)
        x = q_raw[:, cols].astype(F32)
        qh[cols, :] = (x * inverse_rms(x) * q_gain[...]).astype(BF16)
    for h in range(heads):
        load_head(h).wait()

    one = functools.partial(
        first_pass, kv, qh, go, probs, dprobs, block_max, stats, core=core, scale2=scale2
    )
    two = functools.partial(
        second_pass, kv, qh, go, probs, dprobs, block_max, stats, prob_b, dscore_b, dq_t, scale2=scale2
    )

    sibling_copy(z, 1 - core).wait_recv()
    one(zo=z, diagonal=True)

    up_table = {i: d for i, d in enumerate(d for d in GATHER_ORDER if d <= reach)}
    delay = pick(below_top, AROUND_DELAY)
    gather_steps = max(reach, 1 + max((far - d) // 2 + late for d, late in AROUND_DELAY.items() if d <= far))
    word_step = jnp.minimum(2 * (below_top // NEAR), gather_steps)

    def gathered(source, step):
        distance = pick(step, up_table)
        up = z - distance
        around = 2 * (step - delay) + source - 1
        up_valid = jnp.logical_and(distance > 0, up >= 0)
        around_valid = jnp.logical_and(
            below_top <= far, jnp.logical_and(step >= delay, around <= far - below_top)
        )
        owner = jnp.where(source == 0, up, around)
        return owner, jnp.logical_or(
            jnp.logical_and(source == 0, up_valid), jnp.logical_and(source >= 1, around_valid)
        )

    def each_passed_on(source, step, arrival, act):
        owner, comes = gathered(source, step)

        @pl.when(jnp.logical_and(comes, source == 0))
        def _():
            for part in range(2):
                if arrival:
                    up_copy(owner, z - owner, part, z).wait_recv()
                each_up_send(z - owner, part, act)

        @pl.when(jnp.logical_and(comes, source >= 1))
        def _():
            for part in range(2):
                if arrival:
                    around_copy(owner, 0, part, z).wait_recv()
                each_around_send(owner, part, act)

        @pl.when(comes)
        def _():
            act(sibling_copy(owner, core))

    @pl.loop(0, gather_steps + 1)
    def _(step):
        @pl.when(step == word_step)
        def _():
            @pl.when(z + NEAR <= top)
            def _():
                pl.semaphore_wait(word, 1)

            @pl.when(z >= NEAR)
            def _():
                pl.semaphore_signal(word, 1, device_id=chip(z - NEAR), device_id_type=MESH)

        @pl.loop(0, 3)
        def _(source):
            each_passed_on(source, step, True, lambda copy: copy.start())
            owner, comes = gathered(source, step - 1)

            @pl.when(comes)
            def _():
                sibling_copy(owner, 1 - core).wait_recv()
                one(zo=owner, diagonal=False)

    inv_mass = 1.0 / stats[1:2, :]
    stats[2:3, :] = stats[2:3, :] * inv_mass
    stats[1:2, :] = inv_mass
    dq_t[...] = jnp.zeros_like(dq_t)

    order = [d for d in SCATTER_ORDER if d <= reach]
    down_table = {i: d for i, d in enumerate(order)}
    down_table[reach] = 0
    down_parent, wrap_parent = parents(SCATTER, reach), parents(WRAP, far)
    wrap_slot = {c: i for cs in WRAP.values() for i, c in enumerate(cs)}

    def owed(direction, step):
        distance = pick(step, down_table)
        down = z - distance
        around = step if WRAP_UP else z - reach - 1 - step
        owner = jnp.where(direction == 0, down, around)
        limit = jnp.where(direction == 0, distance >= 0, jnp.logical_and(step >= 0, step < z - reach))
        return owner, jnp.logical_and(owner >= 0, limit)

    def swap(owner):
        return pltpu.make_async_remote_copy(
            swap_out.at[owner], swap_in.at[owner], swap_send.at[owner], swap_recv.at[owner],
            device_id={"ctx": sibling}, device_id_type=MESH,
        )

    def down_copy(distance, part, to):
        return pltpu.make_async_remote_copy(
            down_out.at[distance, part], down_in.at[distance, part],
            down_send.at[distance, part], down_recv.at[distance, part],
            device_id=chip(to), device_id_type=MESH,
        )

    def wrap_copy(owner, slot, part, to):
        return pltpu.make_async_remote_copy(
            wrap_out.at[owner, part], wrap_in.at[owner, slot, part],
            wrap_send.at[owner, part], wrap_recv.at[owner, slot, part],
            device_id=chip(to), device_id_type=MESH,
        )

    def add_swapped(step, direction, owner):
        swap(owner).wait_recv()
        for part in range(2):
            keep[step, direction, part, core] += swap_in[owner, part].astype(F32)

    def add_down(step, distance, part):
        for slot in range(2):
            child = pick(distance, children(SCATTER, reach, slot))

            @pl.when(jnp.logical_and(child > 0, z + child - distance <= top))
            def _():
                down_copy(child, part, z).wait_recv()
                keep[step, 0, part, core] += down_in[child, part].astype(F32)

    wrap_children = [pick(below_top, children(WRAP, far, slot)) for slot in range(3)]
    my_slot, my_parent = pick(below_top, wrap_slot), pick(below_top, wrap_parent)

    def add_wrap(step, owner, part):
        for slot in range(3):
            child = wrap_children[slot]

            @pl.when(jnp.logical_and(child > 0, owner <= far - child))
            def _():
                wrap_copy(owner, slot, part, z).wait_recv()
                keep[step, 1, part, core] += wrap_in[owner, slot, part].astype(F32)

    def down_target(distance):
        return z - distance + pick(distance, down_parent)

    def each_wrap_send(owner, part, act):
        for slot in range(3):
            @pl.when(my_slot == slot)
            def _():
                act(wrap_copy(owner, slot, part, top - my_parent))

        @pl.when(below_top == 0)
        def _():
            act(wrap_copy(owner, 0, part, owner))

    def waits_down(distance):
        out = False
        for slot in range(2):
            child = pick(distance, children(SCATTER, reach, slot))
            out = jnp.logical_or(out, jnp.logical_and(child > 0, z + child - distance <= top))
        return out

    def finish_down(step, waiting):
        owner, valid = owed(0, step)
        valid = jnp.logical_and(valid, waits_down(z - owner) == waiting)

        @pl.when(valid)
        def _():
            distance = z - owner
            to = down_target(distance)
            swap(owner).wait_recv()
            for part in range(2):
                if waiting:
                    keep[step, 0, part, core] += swap_in[owner, part].astype(F32)
                    add_down(step, distance, part)
                    down_out[distance, part] = keep[step, 0, part, core].astype(BF16)
                else:
                    both = keep[step, 0, part, core] + swap_in[owner, part].astype(F32)
                    down_out[distance, part] = both.astype(BF16)
                down_copy(distance, part, to).start()

    heights = {(p, e): height(p, e, far) for p in range(far + 1) for e in range(far - p + 1)}
    tallest = max(heights.values())
    limits = []
    for least in range(1, tallest + 1):
        waits = {p: max((e for (q, e), h in heights.items() if q == p and h >= least), default=-1) for p, _ in heights}
        limits.append(pick(below_top, {p: e for p, e in waits.items() if e >= 0}))

    def finish_wrap(now):
        @pl.loop(0, tallest + 1)
        def _(tall):
            step = now - WRAP_LAG[0] - WRAP_LAG[1] * tall
            owner, valid = owed(1, step)

            waits = jnp.int32(0)
            for limit in limits:
                waits += jnp.where(owner <= limit, 1, 0)

            @pl.when(jnp.logical_and(valid, waits == tall))
            def _():
                add_swapped(step, 1, owner)
                for part in range(2):
                    add_wrap(step, owner, part)
                    wrap_out[owner, part] = keep[step, 1, part, core].astype(BF16)
                    each_wrap_send(owner, part, lambda copy: copy.start())

    @pl.loop(0, reach + 1)
    def _(step):
        @pl.loop(0, 2)
        def _(direction):
            owner, valid = owed(direction, step)

            @pl.when(valid)
            def _():
                sums = keep.at[step, direction]
                two(sums=sums, zo=owner)
                for part in range(2):
                    swap_out[owner, part] = sums[part, 1 - core].astype(BF16)
                swap(owner).start()

            @pl.when(direction == 0)
            def _():
                finish_wrap(step)

            @pl.when(direction == 1)
            def _():
                finish_down(step - 1, False)

    q_part = jnp.zeros((1, HD), F32)
    for h in range(heads):
        cols = slice(h * HD, (h + 1) * HD)
        x = q_raw[:, cols].astype(F32)
        q_part += jnp.sum(scale * dq_t[:, cols].T * x * inverse_rms(x), axis=0, keepdims=True)

    def offset(i, count):
        away = (i + 1) // 2
        return count // 2 + jnp.where(i % 2 == 1, -away, away)

    def line_copy(i, slot):
        return pltpu.make_async_remote_copy(
            line_out, line_in.at[slot], line_send.at[i], line_recv.at[slot],
            device_id={"ctx": around_ring(me + offset(i, n), n)}, device_id_type=MESH,
        )

    def plane_copy(i, slot):
        return pltpu.make_async_remote_copy(
            plane_out, plane_in.at[slot], plane_send.at[i], plane_recv.at[slot],
            device_id=plane(around_ring(place + offset(i, group), group)), device_id_type=MESH,
        )

    line_out[...] = q_part
    line_in[me] = q_part

    @pl.loop(0, n - 1)
    def _(i):
        line_copy(i, me).start()

    for h in range(heads):
        cols = slice(h * HD, (h + 1) * HD)
        x = q_raw[:, cols].astype(F32)
        grad, _ = norm_back(x, inverse_rms(x), q_gain[...], scale * dq_t[:, cols].T)
        dq_out[:, cols] = grad.astype(BF16)
    store = pltpu.make_async_copy(dq_out, dq_hbm.at[0], store_sem)
    store.start()

    last = far + 1 + WRAP_LAG[0] + WRAP_LAG[1] * tallest
    @pl.loop(0, max(reach, last))
    def _(step):
        @pl.when(step < reach)
        def _():
            finish_down(step, True)

        @pl.when(step > reach)
        def _():
            finish_wrap(step)

    @pl.loop(0, n - 1)
    def _(i):
        line_copy(i, around_ring(me + offset(i, n), n)).wait_recv()

    plane_out[...] = jnp.sum(line_in[...], axis=0)
    plane_in[place] = plane_out[...]

    @pl.loop(0, group - 1)
    def _(i):
        plane_copy(i, place).start()

    add_swapped(reach, 0, z)
    for part in range(2):
        add_down(reach, 0, part)

    @pl.when(z <= far)
    def _():
        for part in range(2):
            wrap_copy(z, 0, part, z).wait_recv()
            keep[reach, 0, part, core] += wrap_in[z, 0, part].astype(F32)

    x = k_raw[...].astype(F32)
    upstream = scale * keep[reach, 0, 0, core]
    grad, _ = norm_back(x, inverse_rms(x), k_gain[...], upstream)
    dk_out[0] = grad.astype(BF16)
    dv_out[0] = keep[reach, 0, 1, core].astype(BF16)

    def left(copy):
        copy.wait_send()

    each_own_send(left)

    @pl.loop(0, gather_steps)
    def _(step):
        @pl.loop(0, 3)
        def _(source):
            each_passed_on(source, step, False, left)

    @pl.loop(0, reach + 1)
    def _(step):
        owner, valid = owed(0, step)

        @pl.when(valid)
        def _():
            swap(owner).wait_send()

            @pl.when(owner < z)
            def _():
                for part in range(2):
                    down_copy(z - owner, part, down_target(z - owner)).wait_send()

        around, around_valid = owed(1, step)

        @pl.when(around_valid)
        def _():
            swap(around).wait_send()
            for part in range(2):
                each_wrap_send(around, part, left)

    @pl.loop(0, n - 1)
    def _(i):
        line_copy(i, me).wait_send()

    store.wait()

    @pl.loop(0, group - 1)
    def _(i):
        plane_copy(i, around_ring(place + offset(i, group), group)).wait_recv()

    q_total = jnp.sum(plane_in[...], axis=0)
    gains_out[0:1] = q_total
    gains_out[1:2] = q_total * q_gain[...] / k_gain[...]

    @pl.loop(0, group - 1)
    def _(i):
        plane_copy(i, place).wait_send()


def hand_over(*refs):
    count = len(refs) // 2
    for i in range(count):
        refs[count + i][...] = refs[i][...]


def solution(mesh):
    n, tp, dp = mesh.shape["ctx"], mesh.shape["tp"], mesh.shape["dp"]
    chips, reach = n // 2, n // 4
    far = chips - reach - 2

    def shards(q_raw, k_raw, values_in, grad_out, q_gain, k_gain):
        rows, width = q_raw.shape[1:]
        flat = rows * width // HD
        whole = pl.BlockSpec(memory_space=pltpu.VMEM)
        anywhere = pl.BlockSpec(memory_space=pl.ANY)
        dma = pltpu.SemaphoreType.DMA
        outs = pl.pallas_call(
            functools.partial(kernel, n, tp, dp),
            out_shape=(
                jax.ShapeDtypeStruct(q_raw.shape, BF16),
                jax.ShapeDtypeStruct(k_raw.shape, BF16),
                jax.ShapeDtypeStruct(k_raw.shape, BF16),
                jax.ShapeDtypeStruct((2, HD), F32),
            ),
            in_specs=[anywhere] * 4 + [whole] * 2,
            out_specs=(anywhere, whole, whole, whole),
            scratch_shapes=[
                pltpu.VMEM((rows, width), BF16),
                pltpu.VMEM((rows, HD), BF16),
                pltpu.VMEM((flat, HD), BF16),
                pltpu.VMEM((flat, HD), BF16),
                pltpu.VMEM((n, 2, HD, HD), BF16),
                pltpu.VMEM((chips, 2 * HD, flat), F32),
                pltpu.VMEM((chips, 2 * HD, flat), F32),
                pltpu.VMEM((chips, 1, flat), F32),
                pltpu.VMEM((8, flat), F32),
                pltpu.VMEM((2 * HD, flat), BF16),
                pltpu.VMEM((2 * HD, flat), BF16),
                pltpu.VMEM((HD, flat), F32),
                pltpu.VMEM((rows, width), BF16),
                pltpu.VMEM((reach + 1, 2, 2, 2, HD, HD), F32),
                pltpu.VMEM((chips, 2, HD, HD), BF16),
                pltpu.VMEM((chips, 2, HD, HD), BF16),
                pltpu.VMEM((reach + 1, 2, HD, HD), BF16),
                pltpu.VMEM((reach + 1, 2, HD, HD), BF16),
                pltpu.VMEM((far + 1, 2, HD, HD), BF16),
                pltpu.VMEM((far + 1, 3, 2, HD, HD), BF16),
                pltpu.VMEM((1, HD), F32),
                pltpu.VMEM((n, 1, HD), F32),
                pltpu.VMEM((1, HD), F32),
                pltpu.VMEM((tp * dp, 1, HD), F32),
                dma((3,)), dma((flat // HD,)), dma, pltpu.SemaphoreType.REGULAR,
                dma((reach + 1, 2)), dma((reach + 1, 2)),
                dma((far + 1, 2, 2)), dma((far + 1, 2)),
                dma((chips,)), dma((chips,)),
                dma((reach + 1, 2)), dma((reach + 1, 2)),
                dma((far + 1, 2)), dma((far + 1, 3, 2)),
                dma((chips,)), dma((chips,)),
                dma((n,)), dma((n,)),
                dma((tp * dp,)), dma((tp * dp,)),
            ],
            compiler_params=pltpu.CompilerParams(
                collective_id=0, has_side_effects=True, vmem_limit_bytes=60 * 1024 * 1024
            ),
            cost_estimate=pl.CostEstimate(
                flops=10 * flat * n * rows * HD, bytes_accessed=6 * rows * width,
                transcendentals=flat * n * rows,
            ),
        )(q_raw, k_raw, values_in, grad_out, q_gain.reshape(1, HD), k_gain.reshape(1, HD))
        return pl.pallas_call(
            hand_over,
            out_shape=tuple(jax.ShapeDtypeStruct(x.shape, x.dtype) for x in outs),
            in_specs=[whole] * len(outs),
            out_specs=(whole,) * len(outs),
        )(*outs)

    spread = P("dp", "ctx", "tp")
    return jax.shard_map(
        shards,
        mesh=mesh,
        in_specs=(spread, spread, spread, spread, P(), P()),
        out_specs=(spread, spread, spread, P()),
        check_vma=False,
    )
```
